512 devices in a mesh: ctx: 32 (over y_hi, z, core), adp: 16 (over y_lo, x).
Axes of the slice: x: 4, y: 8 (y_hi: 2, y_lo: 4; y = y_hi * 4 + y_lo), z: 8, core: 2. Of those that a mesh axis runs over, the one named last changes fastest.
Arguments:
- queries: bfloat16 [8192, 4096], P('ctx', 'adp'), may hold values from -100 to 100
- keys: bfloat16 [8192, 512], P('ctx'), may hold values from -5 to 5
- values: bfloat16 [8192, 512], P('ctx'), may hold values from -6 to 6
- grad_out: bfloat16 [8192, 4096], P('ctx', 'adp'), may hold values from -6 to 6
- docs: int32 [8192], P('ctx'), may hold values from 0 to 63, never falling along the last dimension, each value on 1 to 6144 neighbouring positions
- block_tenant: int32 [64], P('ctx'), may hold values from 0 to 15
- low_rank: bfloat16 [8192, 64], P('ctx'), may hold values from -6 to 6
- adapter_b: bfloat16 [16, 64, 4096], P('adp'), may hold values from -0.75 to 0.75
Outputs:
- grad_queries: bfloat16 [8192, 4096], P('ctx', 'adp')
- grad_low_rank: float32 [8192, 64], P(('ctx', 'adp'))
- grad_adapter: float32 [16, 64, 4096], P('adp', None, 'ctx')
The draws below stay inside these ranges and needn't reach their ends.
Inputs may be any that keep to these rules, and one draw needn't show every extreme that they name: docs never falls from one position to the next.
All inputs are finite; a program needn't handle non-finite values.
Results may differ from the reference program's by a relative error of at most 0.019.
Values may be sent and summed in bfloat16 or wider, within the bound.
A program may use at most 64 MiB of HBM per device.

```python
import math
import jax
import jax.numpy as jnp
import numpy as np
from jax import lax

QH = 32
KVH = 4
HD = 128
RANK = 64
BLOCK = 128
TOK_DEV = 256
LENGTH = 8192
TENANTS = 16
N_CTX = 32


def aligned_parts(key):
    base = jax.random.normal(jax.random.fold_in(key, 101), (LENGTH, KVH * HD), jnp.float32)
    base = jnp.clip(base, -5.0, 5.0)
    base = base.at[0, 0].set(5.0)
    base = base.at[2, 0].set(-5.0)
    return base


def draw_keys(key, part):
    base = aligned_parts(key)
    return base.astype(jnp.bfloat16)


def draw_queries(key, part):
    fresh = jax.random.normal(jax.random.fold_in(key, 104), (LENGTH, QH * HD), jnp.float32)
    fresh = jnp.clip(fresh, -6.0, 6.0)
    return fresh.astype(jnp.bfloat16)


def set_ends(entries, own_key, least, top_value):
    dims = entries.shape
    index_at = [jax.random.randint(jax.random.fold_in(own_key, axis), (), 0, dims[axis]) for axis in range(len(dims))]
    entries = entries.at[tuple(index_at)].set(least)
    longest = dims.index(max(dims))
    index_at[longest] = (index_at[longest] + 1) % dims[longest]
    return entries.at[tuple(index_at)].set(top_value)


def block_scale(own_key, shape, pieces, least, high):
    def one(position, shards_of):
        steps = jax.random.uniform(jax.random.fold_in(jax.random.fold_in(own_key, 6), position), (shards_of,), jnp.float32, least / len(pieces), high / len(pieces))
        return jnp.repeat(jnp.exp(steps), shape[position] // shards_of).reshape((-1,) + (1,) * (len(shape) - position - 1))

    loudness = one(*pieces[0])
    for cut in pieces[1:]:
        loudness = loudness * one(*cut)
    return loudness


def rank_bounds(amount, slope):
    portions = [(1 << 20) // math.isqrt(rank ** slope) + 1 for rank in range(1, amount + 1)]
    scale = 1 + sum(portions) // (1 << 30)
    return np.cumsum(np.array([max(1, weight // scale) for weight in portions]))


def ranked(key, extent, count, lean):
    listing = rank_bounds(count, lean)
    ticket = jax.random.randint(jax.random.fold_in(key, 1), extent, 0, int(listing[count - 1]))
    standing = jnp.searchsorted(jnp.asarray(listing, jnp.int32), ticket, side="right")
    return jax.random.permutation(jax.random.fold_in(key, 2), count)[standing].astype(jnp.int32)


def split_up(count, total, limit, slope):
    loads = [(1 << 20) // math.isqrt(grade ** slope) + 1 for grade in range(2, count + 1)]
    rest, counts = total - limit - (count - 1), [1] * (count - 1)
    while rest > 0:
        movable = [i for i in range(count - 1) if counts[i] < limit]
        pool, budget = sum([loads[i] for i in movable]), rest
        for i in movable:
            addition = min(limit - counts[i], max(1, budget * loads[i] // pool), rest)
            counts[i] = counts[i] + addition
            rest = rest - addition
    return np.array([limit] + counts)


def uneven_parts(rng, number_of, total, most, slope):
    if number_of == 2:
        one = jax.random.randint(rng, (), max(1, total - most), min(most, total - 1) + 1)
        return jnp.stack([one, total - one])
    tallies = jnp.asarray(split_up(number_of, total, most, slope), jnp.int32)
    couples = (number_of - 1) // 2
    giver, taker = tallies[1:1 + 2 * couples:2], tallies[2:2 + 2 * couples:2]
    slack = jnp.minimum(giver - 1, most - taker)
    passed = jax.random.randint(jax.random.fold_in(rng, 1), (couples,), 0, 1 << 20) % (slack + 1)
    tallies = tallies.at[1:1 + 2 * couples:2].set(giver - passed).at[2:2 + 2 * couples:2].set(taker + passed)
    return tallies[jax.random.permutation(jax.random.fold_in(rng, 2), number_of)]


def bell_draw(stream_key, dims, scale, bound, cuts=(), kind=jnp.bfloat16):
    array = scale * jax.random.normal(stream_key, dims, jnp.float32)
    if cuts:
        array = array * block_scale(stream_key, dims, cuts, -0.22, 0.18)
    return jnp.clip(array, -bound, bound).astype(kind)


def setup_inputs(seed: int = 0) -> dict:
    streams_of = jax.random.split(jax.random.key(seed), 9)
    return {
        "queries": draw_queries(jax.random.fold_in(streams_of[8], 71), 0),
        "keys": draw_keys(jax.random.fold_in(streams_of[8], 71), 0),
        "values": bell_draw(streams_of[2], (LENGTH, KVH * HD), 1.0, 6.0, ((0, 32),)),
        "grad_out": bell_draw(streams_of[3], (LENGTH, QH * HD), 1.0, 6.0, ((0, 32), (1, 16))),
        "docs": jnp.searchsorted(jnp.cumsum(uneven_parts(streams_of[4], 2 * N_CTX, LENGTH, 3 * LENGTH // 4, 0)), jnp.arange(LENGTH), side="right").astype(jnp.int32),
        "block_tenant": set_ends(ranked(streams_of[5], (LENGTH // BLOCK,), TENANTS, 2), jax.random.fold_in(streams_of[5], 3), 0, TENANTS - 1).astype(jnp.int32),
        "low_rank": bell_draw(streams_of[6], (LENGTH, RANK), 1.0, 6.0, ((0, 32),)),
        "adapter_b": bell_draw(streams_of[7], (TENANTS, RANK, QH * HD), RANK ** -0.5, 0.75, ((0, 16),)),
    }


def head_grads(query_head, key_head, value_head, grad_head, docs, positions):
    logit_scale = HD ** -0.5

    def one_block(block_index):
        row_start = (block_index * TOK_DEV).astype(jnp.int32)
        query_block = lax.dynamic_slice_in_dim(query_head, row_start, TOK_DEV, 0)
        grad_block = lax.dynamic_slice_in_dim(grad_head, row_start, TOK_DEV, 0)
        query_pos = lax.dynamic_slice_in_dim(positions, row_start, TOK_DEV, 0)
        query_doc = lax.dynamic_slice_in_dim(docs, row_start, TOK_DEV, 0)
        scores = jnp.dot(query_block, key_head.T, preferred_element_type=jnp.float32) * logit_scale
        visible = (positions[None, :] <= query_pos[:, None]) & (docs[None, :] == query_doc[:, None])
        row_top = jnp.max(jnp.where(visible, scores, -1e30), axis=1)
        row_total = jnp.sum(jnp.where(visible, jnp.exp(scores - row_top[:, None]), 0.0), axis=1)
        log_total = row_top + jnp.log(row_total)
        weights = jnp.where(visible, jnp.exp(scores - log_total[:, None]), 0.0)
        attended = jnp.dot(weights.astype(jnp.bfloat16), value_head, preferred_element_type=jnp.float32)
        row_delta = jnp.sum(grad_block.astype(jnp.float32) * attended, axis=1)
        grad_weights = jnp.dot(grad_block, value_head.T, preferred_element_type=jnp.float32)
        grad_scores = (weights * (grad_weights - row_delta[:, None])).astype(jnp.bfloat16)
        result = jnp.dot(grad_scores, key_head, preferred_element_type=jnp.float32) * logit_scale
        return result.astype(jnp.bfloat16)

    blocks = lax.map(one_block, jnp.arange(LENGTH // TOK_DEV, dtype=jnp.int32))
    return blocks.reshape(LENGTH, HD)


def reference(queries, keys, values, grad_out, docs, block_tenant, low_rank, adapter_b):
    group = QH // KVH
    positions = jnp.arange(LENGTH, dtype=jnp.int32)
    query_heads = queries.reshape(LENGTH, QH, HD).transpose(1, 0, 2)
    grad_heads = grad_out.reshape(LENGTH, QH, HD).transpose(1, 0, 2)
    key_heads = keys.reshape(LENGTH, KVH, HD).transpose(1, 0, 2)
    value_heads = values.reshape(LENGTH, KVH, HD).transpose(1, 0, 2)

    def per_head(head_index):
        kv_index = head_index // group
        return head_grads(query_heads[head_index], key_heads[kv_index], value_heads[kv_index], grad_heads[head_index], docs, positions)

    grads = lax.map(per_head, jnp.arange(QH, dtype=jnp.int32))
    grad_queries = grads.transpose(1, 0, 2).reshape(LENGTH, QH * HD)

    block_count = LENGTH // BLOCK
    grad_blocks = grad_queries.reshape(block_count, BLOCK, QH * HD)
    low_blocks = low_rank.reshape(block_count, BLOCK, RANK)

    def block_step(adapter_acc, inputs):
        grad_block, low_block, tenant = inputs
        chosen = adapter_b[tenant]
        rank_block = jnp.dot(grad_block, chosen.T, preferred_element_type=jnp.float32) * 2.0
        term = jnp.dot(low_block.T, grad_block, preferred_element_type=jnp.float32) * 2.0
        adapter_acc = adapter_acc.at[tenant].add(term)
        return adapter_acc, rank_block

    start_acc = jnp.zeros((TENANTS, RANK, QH * HD), jnp.float32)
    grad_adapter, rank_blocks = lax.scan(block_step, start_acc, (grad_blocks, low_blocks, block_tenant))
    grad_low_rank = rank_blocks.reshape(LENGTH, RANK)
    return grad_queries, grad_low_rank, grad_adapter
```

```python
import math

import jax
import jax.numpy as jnp
from jax import lax
from jax.experimental import pallas as pl
from jax.experimental.pallas import tpu as pltpu
from jax.sharding import PartitionSpec as P

HD = 128
RANK = 64
TOK = 256
NZ = 8
NX = 4
NYL = 4
N_CTX = 32
N_ADP = 16
SLOT = 2 * TOK + 16
EXP2_SCALE = HD ** (-0.5) * math.log2(math.e)
FAR = -1e30
MESH = pl.DeviceIdType.MESH
F32 = jnp.float32
BF16 = jnp.bfloat16


def nt_dot(a, b):
    return lax.dot_general(a, b, (((1,), (1,)), ((), ())), preferred_element_type=F32)


def body(
    q_ref, k_ref, v_ref, go_ref, docs_ref, bt_ref, low_ref, b_ref,
    gq_ref, glr_ref, ga_ref,
    kv, xkv, acc, row_top, qdoc, bcols, btile, lowt,
    pbuf, qbuf, tbuf, gbuf, rsend, rbuf,
    loc_sem, kv_recv, plus_send, minus_send, sib_send, y_send,
    bt_recv, bt_send, b_recv, b_send, bs_recv, bs_send,
    r_recv, r_send, p_recv, p_send, g_recv, g_send,
):
    c = lax.axis_index("ctx")
    a = lax.axis_index("adp")
    core = c % 2
    pair = c // 2
    z = pair % NZ
    y_hi = pair // NZ
    head = a // NX
    x = a % NX
    sib = pair * 2 + (1 - core)
    z_plus = (y_hi * NZ + (z + 1) % NZ) * 2 + core
    z_minus = (y_hi * NZ + (z + NZ - 1) % NZ) * 2 + core
    y_ctx = ((1 - y_hi) * NZ + z) * 2 + core
    y_adp = (NYL - 1 - head) * NX + x
    selfdest = (pair == a).astype(jnp.int32)

    barrier = pltpu.get_barrier_semaphore()

    def greet(ctx, adp):
        pl.semaphore_signal(barrier, inc=1, device_id={"ctx": ctx, "adp": adp}, device_id_type=MESH)

    greet(y_ctx, y_adp)

    @pl.loop(1, N_CTX)
    def _(i):
        greet((c + i) % N_CTX, a)

    @pl.loop(1, N_ADP)
    def _(i):
        greet(c, (a + i) % N_ADP)

    @pl.loop(0, N_ADP)
    def _(i):
        @pl.when(jnp.logical_not((pair == a) & (i == pair)))
        def _():
            greet(i * 2 + core, pair)

    def col(which):
        return pl.ds(pl.multiple_of(which * HD, HD), HD)

    own_k = pltpu.make_async_copy(k_ref.at[:, col(head)], kv.at[c, pl.ds(0, TOK)], loc_sem.at[0])
    own_v = pltpu.make_async_copy(v_ref.at[:, col(head)], kv.at[c, pl.ds(TOK, TOK)], loc_sem.at[1])
    other = NYL - 1 - head
    x_k = pltpu.make_async_copy(k_ref.at[:, col(other)], xkv.at[pl.ds(0, TOK)], loc_sem.at[2])
    x_v = pltpu.make_async_copy(v_ref.at[:, col(other)], xkv.at[pl.ds(TOK, TOK)], loc_sem.at[3])
    half = pl.multiple_of(core * (RANK // 2), RANK // 2)
    own_b = pltpu.make_async_copy(
        b_ref.at[0, pl.ds(half, RANK // 2), pl.ds(pl.multiple_of(a * 2 * HD, 2 * HD), 2 * HD)],
        bcols.at[a, pl.ds(half, RANK // 2)],
        loc_sem.at[4],
    )
    own_k.start()
    own_v.start()
    x_k.start()
    x_v.start()
    own_b.start()

    doc_rows = docs_ref[...].astype(F32)
    tag = jnp.concatenate([doc_rows, jnp.zeros((14, HD), F32)], axis=0).astype(BF16)
    kv[c, pl.ds(2 * TOK, 16), :] = tag
    xkv[pl.ds(2 * TOK, 16), :] = tag
    sub8 = lax.broadcasted_iota(jnp.int32, (8, HD), 0)
    btile[c] = jnp.where(sub8 < 4, bt_ref[0], bt_ref[1])

    own_k.wait()
    own_v.wait()
    x_k.wait()
    x_v.wait()
    own_b.wait()
    pl.semaphore_wait(barrier, 1 + (N_CTX - 1) + (N_ADP - 1) + N_ADP - selfdest)

    def move(chunk, send_sem, to):
        return pltpu.make_async_remote_copy(
            src_ref=kv.at[chunk], dst_ref=kv.at[chunk],
            send_sem=send_sem.at[chunk], recv_sem=kv_recv.at[chunk],
            device_id={"ctx": to, "adp": a}, device_id_type=MESH,
        )

    def to_y():
        return pltpu.make_async_remote_copy(
            src_ref=xkv, dst_ref=kv.at[c], send_sem=y_send, recv_sem=kv_recv.at[c],
            device_id={"ctx": y_ctx, "adp": y_adp}, device_id_type=MESH,
        )

    move(c, plus_send, z_plus).start()
    move(c, minus_send, z_minus).start()
    move(c, sib_send, sib).start()

    @pl.when(y_hi == 0)
    def _():
        to_y().start()

    def bt_copy(i):
        to = (c + i) % N_CTX
        return pltpu.make_async_remote_copy(
            src_ref=btile.at[c], dst_ref=btile.at[c], send_sem=bt_send.at[to], recv_sem=bt_recv.at[c],
            device_id={"ctx": to, "adp": a}, device_id_type=MESH,
        )

    def bt_arrival(i):
        frm = (c + i) % N_CTX
        return pltpu.make_async_copy(btile.at[frm], btile.at[frm], bt_recv.at[frm])

    def b_copy(i):
        to = (a + i) % N_ADP
        return pltpu.make_async_remote_copy(
            src_ref=b_ref.at[0, pl.ds(half, RANK // 2), pl.ds(pl.multiple_of(to * 2 * HD, 2 * HD), 2 * HD)],
            dst_ref=bcols.at[a, pl.ds(half, RANK // 2)],
            send_sem=b_send.at[to], recv_sem=b_recv.at[a],
            device_id={"ctx": c, "adp": to}, device_id_type=MESH,
        )

    def b_arrival(i):
        frm = (a + i) % N_ADP
        ref = bcols.at[frm, pl.ds(half, RANK // 2)]
        return pltpu.make_async_copy(ref, ref, b_recv.at[frm])

    def b_share():
        ref = bcols.at[:, pl.ds(half, RANK // 2)]
        return pltpu.make_async_remote_copy(
            src_ref=ref, dst_ref=ref, send_sem=bs_send, recv_sem=bs_recv,
            device_id={"ctx": sib, "adp": a}, device_id_type=MESH,
        )

    def b_shared():
        ref = bcols.at[:, pl.ds(pl.multiple_of((1 - core) * (RANK // 2), RANK // 2), RANK // 2)]
        return pltpu.make_async_copy(ref, ref, bs_recv)

    @pl.loop(1, N_CTX)
    def _(i):
        bt_copy(i).start()

    @pl.loop(1, N_ADP)
    def _(i):
        b_copy(i).start()

    rr = lax.broadcasted_iota(jnp.int32, (2 * RANK, RANK), 0)
    kk = lax.broadcasted_iota(jnp.int32, (2 * RANK, RANK), 1)
    pick = jnp.where(kk == ((rr >> 3) * 4 + (rr & 3)), 1.0, 0.0).astype(BF16)
    spread = nt_dot(pick, low_ref[...])
    rr = lax.broadcasted_iota(jnp.int32, (2 * RANK, TOK), 0)
    tt = lax.broadcasted_iota(jnp.int32, (2 * RANK, TOK), 1)
    lowt[...] = jnp.where((tt >> 7) == ((rr >> 2) & 1), spread, 0.0).astype(BF16)

    ri = lax.broadcasted_iota(jnp.int32, (HD, HD), 0)
    ci = lax.broadcasted_iota(jnp.int32, (HD, HD), 1)
    for part in range(2):
        spot = jnp.where(ri == ci, jnp.broadcast_to(doc_rows[part : part + 1, :], (HD, HD)), 0.0)
        column = jnp.sum(spot, axis=1, keepdims=True)
        qdoc[pl.ds(part * HD, HD), :] = jnp.broadcast_to(column, (HD, HD))

    ones = jnp.ones((TOK, HD), BF16)

    def attend(which, first):
        low_slot = which * 2
        row_doc = qdoc[...]
        for h in range(2):
            q_h = q_ref[:, h * HD : (h + 1) * HD]
            g_h = go_ref[:, h * HD : (h + 1) * HD]
            tiles = []
            for half_pair in range(2):
                scores = nt_dot(q_h, kv[low_slot + half_pair, pl.ds(0, TOK), :])
                key_doc = kv[low_slot + half_pair, pl.ds(2 * TOK, 16), :].astype(F32)
                for lt in range(2):
                    seen = row_doc == key_doc[lt : lt + 1, :]
                    if first:
                        rpos = lax.broadcasted_iota(jnp.int32, (TOK, HD), 0) + core * TOK
                        kpos = lax.broadcasted_iota(jnp.int32, (TOK, HD), 1) + (half_pair * TOK + lt * HD)
                        seen = seen & (kpos <= rpos)
                    tiles.append(jnp.where(seen, scores[:, lt * HD : (lt + 1) * HD], FAR))
            top = jnp.maximum(jnp.maximum(tiles[0], tiles[1]), jnp.maximum(tiles[2], tiles[3]))
            top = jnp.broadcast_to(jnp.max(top, axis=1, keepdims=True), (TOK, HD))
            if not first:
                before = row_top[h]
                top = jnp.maximum(top, before)
                decay = jnp.exp2((before - top) * EXP2_SCALE)
            row_top[h] = top
            total = None
            for half_pair in range(2):
                weights = [
                    jnp.exp2((tiles[half_pair * 2 + lt] - top) * EXP2_SCALE) for lt in range(2)
                ]
                weights = jnp.concatenate(weights, axis=1)
                gw = nt_dot(g_h, kv[low_slot + half_pair, pl.ds(TOK, TOK), :])
                both = jnp.concatenate([weights.astype(BF16), (weights * gw).astype(BF16)], axis=0)
                right = jnp.concatenate([kv[low_slot + half_pair, pl.ds(0, TOK), :], ones], axis=1)
                term = jnp.dot(both, right, preferred_element_type=F32)
                total = term if total is None else total + term
            if first:
                acc[h] = total
            else:
                wide = jnp.concatenate([decay, decay], axis=1)
                wide = jnp.concatenate([wide, wide], axis=0)
                acc[h] = acc[h] * wide + total

    def arrived(chunk):
        pltpu.make_async_copy(kv.at[chunk], kv.at[chunk], kv_recv.at[chunk]).wait()

    arrived(sib)
    attend(pair, True)

    def event(e):
        s, u = e // 4, e % 4
        lower, back = u // 2, u % 2
        dist = s - lower
        valid = (dist >= 0) & (lower <= y_hi)
        valid = valid & ((dist > 0) | ((lower == 1) & (back == 0)))
        valid = valid & ((dist <= 3) | ((dist == 4) & (back != lower)))
        from_z = (z + NZ - dist + 2 * dist * back) % NZ
        src_pair = jnp.where(lower == 1, 0, y_hi) * NZ + from_z
        on_plus = valid & ((back == 0) | (dist == 0)) & ((dist <= 2) | ((dist == 3) & (lower == 1)))
        on_minus = valid & ((back == 1) | (dist == 0)) & ((dist <= 2) | ((dist == 3) & (lower == 0)))
        return valid, src_pair, on_plus, on_minus

    @pl.loop(4, 24)
    def _(e):
        valid, src_pair, on_plus, on_minus = event(e)
        chunk = src_pair * 2 + core

        @pl.when(valid)
        def _():
            arrived(chunk)

            @pl.when(on_plus)
            def _():
                move(chunk, plus_send, z_plus).start()

            @pl.when(on_minus)
            def _():
                move(chunk, minus_send, z_minus).start()

            move(chunk, sib_send, sib).start()
            arrived(src_pair * 2 + 1 - core)

            @pl.when(src_pair < pair)
            def _():
                attend(src_pair, False)

    @pl.loop(1, N_ADP)
    def _(i):
        b_arrival(i).wait()

    b_share().start()

    for h in range(2):
        total = acc[h, pl.ds(0, TOK), pl.ds(HD, HD)]
        inv = 1.0 / total
        delta = acc[h, pl.ds(TOK, TOK), pl.ds(HD, HD)] * inv
        grad = (acc[h, pl.ds(TOK, TOK), pl.ds(0, HD)] - delta * acc[h, pl.ds(0, TOK), pl.ds(0, HD)]) * inv
        gq_ref[:, h * HD : (h + 1) * HD] = (grad * HD ** (-0.5)).astype(BF16)

    gq = gq_ref[...]
    partial = jnp.dot(lowt[...], gq, preferred_element_type=F32) * 2.0
    for h in range(2):
        pbuf[h] = partial[:, h * HD : (h + 1) * HD].reshape(N_ADP, 8, HD)

    def p_copy(i):
        to = (c + i) % N_CTX
        return pltpu.make_async_remote_copy(
            src_ref=pbuf.at[to % 2, to // 2], dst_ref=qbuf.at[c],
            send_sem=p_send.at[to], recv_sem=p_recv.at[c],
            device_id={"ctx": to, "adp": a}, device_id_type=MESH,
        )

    def p_arrival(i):
        frm = (c + i) % N_CTX
        return pltpu.make_async_copy(qbuf.at[frm], qbuf.at[frm], p_recv.at[frm])

    @pl.loop(1, N_CTX)
    def _(i):
        p_copy(i).start()

    qbuf[c] = pbuf[core, pair]

    b_shared().wait()
    b_share().wait_send()
    for blk in range(2):
        chosen = bcols[bt_ref[blk]]
        padded = jnp.concatenate([chosen, jnp.zeros_like(chosen)], axis=0)
        part = nt_dot(gq[blk * HD : (blk + 1) * HD, :], padded) * 2.0
        rsend[pl.ds(blk * 8, 8)] = part.reshape(8, 16, HD)

    def r_copy(i):
        to = (a + i) % N_ADP
        return pltpu.make_async_remote_copy(
            src_ref=rsend.at[to], dst_ref=rbuf.at[a], send_sem=r_send.at[to], recv_sem=r_recv.at[a],
            device_id={"ctx": c, "adp": to}, device_id_type=MESH,
        )

    def r_arrival(i):
        frm = (a + i) % N_ADP
        return pltpu.make_async_copy(rbuf.at[frm], rbuf.at[frm], r_recv.at[frm])

    @pl.loop(1, N_ADP)
    def _(i):
        r_copy(i).start()

    rbuf[a] = rsend[a]

    @pl.loop(1, N_CTX)
    def _(i):
        bt_arrival(i).wait()
        p_arrival(i).wait()

    def add_source(i, sums):
        tile, owner = qbuf[i], btile[i]
        return tuple(s + jnp.where(owner == t, tile, 0.0) for t, s in enumerate(sums))

    sums = lax.fori_loop(0, N_CTX, add_source, tuple(jnp.zeros((8, HD), F32) for _ in range(N_ADP)))
    for t in range(N_ADP):
        tbuf[t] = sums[t]

    def g_copy(t):
        return pltpu.make_async_remote_copy(
            src_ref=tbuf.at[t], dst_ref=gbuf.at[pair], send_sem=g_send.at[t], recv_sem=g_recv.at[pair],
            device_id={"ctx": a * 2 + core, "adp": t}, device_id_type=MESH,
        )

    def g_arrival(i):
        return pltpu.make_async_copy(gbuf.at[i], gbuf.at[i], g_recv.at[i])

    def not_self(i):
        return jnp.logical_not((pair == a) & (i == a))

    @pl.loop(0, N_ADP)
    def _(i):
        t = (a + i) % N_ADP

        @pl.when(not_self(t))
        def _():
            g_copy(t).start()

    @pl.when(pair == a)
    def _():
        gbuf[pair] = tbuf[a]

    @pl.loop(1, N_ADP)
    def _(i):
        r_arrival(i).wait()

    share = rbuf[0]
    for i in range(1, N_ADP):
        share = share + rbuf[i]
    glr_ref[...] = share[:, :RANK]

    @pl.loop(0, N_ADP)
    def _(i):
        @pl.when(not_self(i))
        def _():
            g_arrival(i).wait()

    for i in range(N_ADP):
        tile = gbuf[i]
        ga_ref[0, pl.ds(i * 4, 4), :] = tile[0:4] + tile[4:8]

    move(c, plus_send, z_plus).wait_send()
    move(c, minus_send, z_minus).wait_send()
    move(c, sib_send, sib).wait_send()

    @pl.when(y_hi == 0)
    def _():
        to_y().wait_send()

    @pl.loop(4, 24)
    def _(e):
        valid, src_pair, on_plus, on_minus = event(e)
        chunk = src_pair * 2 + core

        @pl.when(on_plus)
        def _():
            move(chunk, plus_send, z_plus).wait_send()

        @pl.when(on_minus)
        def _():
            move(chunk, minus_send, z_minus).wait_send()

        @pl.when(valid)
        def _():
            move(chunk, sib_send, sib).wait_send()

    @pl.loop(1, N_CTX)
    def _(i):
        bt_copy(i).wait_send()
        p_copy(i).wait_send()

    @pl.loop(1, N_ADP)
    def _(i):
        b_copy(i).wait_send()
        r_copy(i).wait_send()

    @pl.loop(0, N_ADP)
    def _(i):
        @pl.when(not_self(i))
        def _():
            g_copy(i).wait_send()


def on_device(queries, keys, values, grad_out, docs, block_tenant, low_rank, adapter_b):
    vmem = pl.BlockSpec(memory_space=pltpu.VMEM)
    anywhere = pl.BlockSpec(memory_space=pl.ANY)
    dma = pltpu.SemaphoreType.DMA
    return pl.pallas_call(
        body,
        out_shape=(
            jax.ShapeDtypeStruct((TOK, 2 * HD), BF16),
            jax.ShapeDtypeStruct((16, RANK), F32),
            jax.ShapeDtypeStruct((1, RANK, HD), F32),
        ),
        in_specs=[
            vmem, anywhere, anywhere, vmem, vmem,
            pl.BlockSpec(memory_space=pltpu.SMEM), vmem, anywhere,
        ],
        out_specs=(vmem, vmem, vmem),
        scratch_shapes=[
            pltpu.VMEM((N_CTX, SLOT, HD), BF16),
            pltpu.VMEM((SLOT, HD), BF16),
            pltpu.VMEM((2, 2 * TOK, 2 * HD), F32),
            pltpu.VMEM((2, TOK, HD), F32),
            pltpu.VMEM((TOK, HD), F32),
            pltpu.VMEM((N_ADP, RANK, 2 * HD), BF16),
            pltpu.VMEM((N_CTX, 8, HD), jnp.int32),
            pltpu.VMEM((2 * RANK, TOK), BF16),
            pltpu.VMEM((2, N_ADP, 8, HD), F32),
            pltpu.VMEM((N_CTX, 8, HD), F32),
            pltpu.VMEM((N_ADP, 8, HD), F32),
            pltpu.VMEM((N_ADP, 8, HD), F32),
            pltpu.VMEM((N_ADP, 16, HD), F32),
            pltpu.VMEM((N_ADP, 16, HD), F32),
            dma((5,)), dma((N_CTX,)), dma((N_CTX,)), dma((N_CTX,)), dma((N_CTX,)), dma,
            dma((N_CTX,)), dma((N_CTX,)), dma((N_ADP,)), dma((N_ADP,)), dma, dma,
            dma((N_ADP,)), dma((N_ADP,)), dma((N_CTX,)), dma((N_CTX,)), dma((N_ADP,)), dma((N_ADP,)),
        ],
        compiler_params=pltpu.CompilerParams(
            collective_id=0, has_side_effects=True, vmem_limit_bytes=48 * 1024 * 1024
        ),
        cost_estimate=pl.CostEstimate(flops=4_000_000_000, bytes_accessed=4_000_000, transcendentals=4_000_000),
    )(
        queries, keys, values, grad_out, docs.reshape(2, HD), block_tenant, low_rank, adapter_b
    )


def solution(mesh):
    placed = (
        P("ctx", "adp"),
        P("ctx", None),
        P("ctx", None),
        P("ctx", "adp"),
        P("ctx"),
        P("ctx"),
        P("ctx", None),
        P("adp", None, None),
    )
    return jax.shard_map(
        on_device,
        mesh=mesh,
        in_specs=placed,
        out_specs=(P("ctx", "adp"), P(("ctx", "adp"), None), P("adp", None, "ctx")),
        check_vma=False,
    )
```

```python
import math

import jax
import jax.numpy as jnp
from jax import lax
from jax.experimental import pallas as pl
from jax.experimental.pallas import tpu as pltpu
from jax.sharding import PartitionSpec as P

HD = 128
RANK = 64
TOK = 256
NZ = 8
NX = 4
NYL = 4
N_CTX = 32
N_ADP = 16
SLOT = TOK + 16
HALF = TOK // 2
EXP2_SCALE = HD ** (-0.5) * math.log2(math.e)
FAR = -1e30
MESH = pl.DeviceIdType.MESH
F32 = jnp.float32
BF16 = jnp.bfloat16


def nt_dot(a, b):
    return lax.dot_general(a, b, (((1,), (1,)), ((), ())), preferred_element_type=F32)


def body(
    q_hbm, k_hbm, v_hbm, go_hbm, docs_hbm, bt_hbm, low_hbm, b_hbm,
    gq_hbm, glr_hbm, ga_hbm,
    kv, xkv, q_ref, go_ref, docs_ref, bt_ref, low_ref, gq_ref, glr_ref, ga_ref,
    acc, row_top, qdoc, bcols, btile, lowt, pbuf, qbuf, tbuf, gbuf, rsend, rbuf,
    loc_sem, mine_recv, other_recv, plus_send, minus_send, sib_send, sib2_send, x_send, y_send,
    bt_recv, bt_send, b_recv, b_send, bs_recv, bs_send,
    r_recv, r_send, p_recv, p_send, g_recv, g_send, out_sem,
):
    c = lax.axis_index("ctx")
    a = lax.axis_index("adp")
    core = c % 2
    pair = c // 2
    z = pair % NZ
    y_hi = pair // NZ
    head = a // NX
    x = a % NX
    mine = x % 2
    other = 1 - mine
    sib = pair * 2 + (1 - core)
    z_plus = (y_hi * NZ + (z + 1) % NZ) * 2 + core
    z_minus = (y_hi * NZ + (z + NZ - 1) % NZ) * 2 + core
    x_plus = head * NX + (x + 1) % NX
    x_minus = head * NX + (x + NX - 1) % NX
    y_ctx = ((1 - y_hi) * NZ + z) * 2 + core
    y_adp = (NYL - 1 - head) * NX + x
    selfdest = (pair == a).astype(jnp.int32)

    barrier = pltpu.get_barrier_semaphore()

    def greet(ctx, adp):
        pl.semaphore_signal(barrier, inc=1, device_id={"ctx": ctx, "adp": adp}, device_id_type=MESH)

    greet(y_ctx, y_adp)

    @pl.loop(1, N_CTX)
    def _(i):
        greet((c + i) % N_CTX, a)

    @pl.loop(1, N_ADP)
    def _(i):
        greet(c, (a + i) % N_ADP)

    @pl.loop(0, N_ADP)
    def _(i):
        @pl.when(jnp.logical_not((pair == a) & (i == pair)))
        def _():
            greet(i * 2 + core, pair)

    def col(which):
        return pl.ds(pl.multiple_of(which * HD, HD), HD)

    far_head = NYL - 1 - head
    get_docs = pltpu.make_async_copy(docs_hbm, docs_ref, loc_sem.at[0])
    own_k = pltpu.make_async_copy(k_hbm.at[:, col(head)], kv.at[c, 0, pl.ds(0, TOK)], loc_sem.at[1])
    own_v = pltpu.make_async_copy(v_hbm.at[:, col(head)], kv.at[c, 1, pl.ds(0, TOK)], loc_sem.at[2])
    x_k = pltpu.make_async_copy(k_hbm.at[:, col(far_head)], xkv.at[pl.ds(0, TOK)], loc_sem.at[3])
    x_v = pltpu.make_async_copy(v_hbm.at[:, col(far_head)], xkv.at[pl.ds(0, TOK)], loc_sem.at[3])
    get_q = pltpu.make_async_copy(q_hbm, q_ref, loc_sem.at[4])
    get_go = pltpu.make_async_copy(go_hbm, go_ref, loc_sem.at[5])
    get_bt = pltpu.make_async_copy(bt_hbm, bt_ref, loc_sem.at[6])
    get_low = pltpu.make_async_copy(low_hbm, low_ref, loc_sem.at[7])
    half = pl.multiple_of(core * (RANK // 2), RANK // 2)
    own_b = pltpu.make_async_copy(
        b_hbm.at[0, pl.ds(half, RANK // 2), pl.ds(pl.multiple_of(a * 2 * HD, 2 * HD), 2 * HD)],
        bcols.at[a, pl.ds(half, RANK // 2)],
        loc_sem.at[8],
    )
    get_docs.start()
    own_k.start()
    own_v.start()

    @pl.when(mine == 0)
    def _():
        x_k.start()

    @pl.when(mine == 1)
    def _():
        x_v.start()

    get_bt.start()
    get_q.start()
    get_go.start()
    get_low.start()
    own_b.start()

    get_docs.wait()
    doc_rows = docs_ref[...].astype(F32)
    tag = jnp.concatenate([doc_rows, jnp.zeros((14, HD), F32)], axis=0).astype(BF16)
    kv[c, mine, pl.ds(TOK, 16), :] = tag
    xkv[pl.ds(TOK, 16), :] = tag
    own_k.wait()
    own_v.wait()
    x_k.wait()
    pl.semaphore_wait(barrier, 1 + (N_CTX - 1) + (N_ADP - 1) + N_ADP - selfdest)

    def along(chunk, send_sem, to):
        ref = kv.at[chunk, mine]
        return pltpu.make_async_remote_copy(
            src_ref=ref, dst_ref=ref, send_sem=send_sem.at[chunk], recv_sem=mine_recv.at[chunk],
            device_id={"ctx": to, "adp": a}, device_id_type=MESH,
        )

    def rest_to_sib(chunk):
        ref = kv.at[chunk, other, pl.ds(0, TOK)]
        return pltpu.make_async_remote_copy(
            src_ref=ref, dst_ref=ref, send_sem=sib2_send.at[chunk], recv_sem=other_recv.at[chunk],
            device_id={"ctx": sib, "adp": a}, device_id_type=MESH,
        )

    def swap(chunk, first, to):
        ref = kv.at[chunk, mine, pl.ds(first, HALF)]
        return pltpu.make_async_remote_copy(
            src_ref=ref, dst_ref=ref, send_sem=x_send.at[chunk], recv_sem=other_recv.at[chunk],
            device_id={"ctx": c, "adp": to}, device_id_type=MESH,
        )

    def to_y():
        return pltpu.make_async_remote_copy(
            src_ref=xkv, dst_ref=kv.at[c, mine], send_sem=y_send, recv_sem=mine_recv.at[c],
            device_id={"ctx": y_ctx, "adp": y_adp}, device_id_type=MESH,
        )

    def await_mine(chunk):
        ref = kv.at[chunk, mine]
        pltpu.make_async_copy(ref, ref, mine_recv.at[chunk]).wait()

    def await_other(chunk):
        ref = kv.at[chunk, other, pl.ds(0, TOK)]
        pltpu.make_async_copy(ref, ref, other_recv.at[chunk]).wait()

    def await_swap_sent(chunk):
        ref = kv.at[chunk, mine, pl.ds(0, TOK)]
        pltpu.make_async_copy(ref, ref, x_send.at[chunk]).wait()

    along(c, plus_send, z_plus).start()
    along(c, minus_send, z_minus).start()

    @pl.when(y_hi == 0)
    def _():
        to_y().start()

    along(c, sib_send, sib).start()
    rest_to_sib(c).start()

    def b_copy(i):
        to = (a + i) % N_ADP
        return pltpu.make_async_remote_copy(
            src_ref=b_hbm.at[0, pl.ds(half, RANK // 2), pl.ds(pl.multiple_of(to * 2 * HD, 2 * HD), 2 * HD)],
            dst_ref=bcols.at[a, pl.ds(half, RANK // 2)],
            send_sem=b_send, recv_sem=b_recv,
            device_id={"ctx": c, "adp": to}, device_id_type=MESH,
        )

    def b_all(sem):
        ref = bcols.at[pl.ds(0, N_ADP - 1), pl.ds(half, RANK // 2)]
        return pltpu.make_async_copy(ref, ref, sem)

    def b_share():
        ref = bcols.at[:, pl.ds(half, RANK // 2)]
        return pltpu.make_async_remote_copy(
            src_ref=ref, dst_ref=ref, send_sem=bs_send, recv_sem=bs_recv,
            device_id={"ctx": sib, "adp": a}, device_id_type=MESH,
        )

    def b_shared():
        ref = bcols.at[:, pl.ds(pl.multiple_of((1 - core) * (RANK // 2), RANK // 2), RANK // 2)]
        return pltpu.make_async_copy(ref, ref, bs_recv)

    @pl.loop(1, N_ADP)
    def _(i):
        b_copy(i).start()

    get_bt.wait()
    btile[c] = jnp.where(lax.broadcasted_iota(jnp.int32, (2, HD), 0) == 0, bt_ref[0], bt_ref[1])

    def bt_copy(i):
        to = (c + i) % N_CTX
        return pltpu.make_async_remote_copy(
            src_ref=btile.at[c], dst_ref=btile.at[c], send_sem=bt_send, recv_sem=bt_recv,
            device_id={"ctx": to, "adp": a}, device_id_type=MESH,
        )

    def bt_all(sem):
        ref = btile.at[pl.ds(0, N_CTX - 1)]
        return pltpu.make_async_copy(ref, ref, sem)

    @pl.loop(1, N_CTX)
    def _(i):
        bt_copy(i).start()

    get_low.wait()
    rr = lax.broadcasted_iota(jnp.int32, (2 * RANK, RANK), 0)
    kk = lax.broadcasted_iota(jnp.int32, (2 * RANK, RANK), 1)
    pick = jnp.where(kk == ((rr >> 3) * 4 + (rr & 3)), 1.0, 0.0).astype(BF16)
    spread = jnp.dot(pick, low_ref[...], preferred_element_type=F32)
    rr = lax.broadcasted_iota(jnp.int32, (2 * RANK, TOK), 0)
    tt = lax.broadcasted_iota(jnp.int32, (2 * RANK, TOK), 1)
    lowt[...] = jnp.where((tt >> 7) == ((rr >> 2) & 1), spread, 0.0).astype(BF16)

    ri = lax.broadcasted_iota(jnp.int32, (HD, HD), 0)
    ci = lax.broadcasted_iota(jnp.int32, (HD, HD), 1)
    for part in range(2):
        spot = jnp.where(ri == ci, jnp.broadcast_to(doc_rows[part : part + 1, :], (HD, HD)), 0.0)
        column = jnp.sum(spot, axis=1, keepdims=True)
        qdoc[pl.ds(part * HD, HD), :] = jnp.broadcast_to(column, (HD, HD))

    ones = jnp.ones((TOK, HD), BF16)

    def attend(which, first):
        low_slot = which * 2
        row_doc = qdoc[...]
        for h in range(2):
            q_h = q_ref[:, h * HD : (h + 1) * HD]
            g_h = go_ref[:, h * HD : (h + 1) * HD]
            tiles = []
            for half_pair in range(2):
                scores = nt_dot(q_h, kv[low_slot + half_pair, 0, pl.ds(0, TOK), :])
                key_doc = kv[low_slot + half_pair, mine, pl.ds(TOK, 16), :].astype(F32)
                for lt in range(2):
                    seen = row_doc == key_doc[lt : lt + 1, :]
                    if first:
                        rpos = lax.broadcasted_iota(jnp.int32, (TOK, HD), 0) + core * TOK
                        kpos = lax.broadcasted_iota(jnp.int32, (TOK, HD), 1) + (half_pair * TOK + lt * HD)
                        seen = seen & (kpos <= rpos)
                    tiles.append(jnp.where(seen, scores[:, lt * HD : (lt + 1) * HD], FAR))
            top = jnp.maximum(jnp.maximum(tiles[0], tiles[1]), jnp.maximum(tiles[2], tiles[3]))
            top = jnp.broadcast_to(jnp.max(top, axis=1, keepdims=True), (TOK, HD))
            if not first:
                before = row_top[h]
                top = jnp.maximum(top, before)
                decay = jnp.exp2((before - top) * EXP2_SCALE)
            row_top[h] = top
            total = None
            for half_pair in range(2):
                weights = [
                    jnp.exp2((tiles[half_pair * 2 + lt] - top) * EXP2_SCALE) for lt in range(2)
                ]
                weights = jnp.concatenate(weights, axis=1)
                gw = nt_dot(g_h, kv[low_slot + half_pair, 1, pl.ds(0, TOK), :])
                both = jnp.concatenate([weights.astype(BF16), (weights * gw).astype(BF16)], axis=0)
                right = jnp.concatenate([kv[low_slot + half_pair, 0, pl.ds(0, TOK), :], ones], axis=1)
                term = jnp.dot(both, right, preferred_element_type=F32)
                total = term if total is None else total + term
            if first:
                acc[h] = total
            else:
                wide = jnp.concatenate([decay, decay], axis=1)
                wide = jnp.concatenate([wide, wide], axis=0)
                acc[h] = acc[h] * wide + total

    get_q.wait()
    get_go.wait()
    await_mine(sib)
    await_other(sib)
    attend(pair, True)

    def event(e):
        s, u = e // 4, e % 4
        lower, back = u // 2, u % 2
        dist = s - lower
        valid = (dist >= 0) & (lower <= y_hi)
        valid = valid & ((dist > 0) | ((lower == 1) & (back == 0)))
        valid = valid & ((dist <= 3) | ((dist == 4) & (back != lower)))
        from_z = (z + NZ - dist + 2 * dist * back) % NZ
        src_pair = jnp.where(lower == 1, 0, y_hi) * NZ + from_z
        on_plus = valid & ((back == 0) | (dist == 0)) & ((dist <= 2) | ((dist == 3) & (lower == 1)))
        on_minus = valid & ((back == 1) | (dist == 0)) & ((dist <= 2) | ((dist == 3) & (lower == 0)))
        return valid, src_pair, on_plus, on_minus

    @pl.loop(4, 25)
    def _(e):
        valid, src_pair, on_plus, on_minus = event(e)
        chunk = src_pair * 2 + core

        @pl.when(valid)
        def _():
            await_mine(chunk)

            @pl.when(on_plus)
            def _():
                along(chunk, plus_send, z_plus).start()

            @pl.when(on_minus)
            def _():
                along(chunk, minus_send, z_minus).start()

            swap(chunk, 0, x_plus).start()
            swap(chunk, HALF, x_minus).start()
            along(chunk, sib_send, sib).start()

        ready, src_pair, _, _ = event(e - 1)
        chunk2 = src_pair * 2 + core

        @pl.when(ready)
        def _():
            await_other(chunk2)
            rest_to_sib(chunk2).start()

        whole, last_pair, _, _ = event(e - 2)

        @pl.when(whole)
        def _():
            await_mine(last_pair * 2 + 1 - core)
            await_other(last_pair * 2 + 1 - core)

        @pl.when(whole & (last_pair < pair))
        def _():
            attend(last_pair, False)

    b_all(b_recv).wait()
    own_b.wait()
    b_share().start()

    for h in range(2):
        total = acc[h, pl.ds(0, TOK), pl.ds(HD, HD)]
        inv = 1.0 / total
        delta = acc[h, pl.ds(TOK, TOK), pl.ds(HD, HD)] * inv
        grad = (acc[h, pl.ds(TOK, TOK), pl.ds(0, HD)] - delta * acc[h, pl.ds(0, TOK), pl.ds(0, HD)]) * inv
        gq_ref[:, h * HD : (h + 1) * HD] = (grad * HD ** (-0.5)).astype(BF16)

    gq = gq_ref[...]
    partial = jnp.dot(lowt[...], gq, preferred_element_type=F32) * 2.0
    for h in range(2):
        pbuf[h] = partial[:, h * HD : (h + 1) * HD].reshape(N_ADP, 8, HD)

    def p_copy(i):
        to = (c + i) % N_CTX
        return pltpu.make_async_remote_copy(
            src_ref=pbuf.at[to % 2, to // 2], dst_ref=qbuf.at[c],
            send_sem=p_send, recv_sem=p_recv,
            device_id={"ctx": to, "adp": a}, device_id_type=MESH,
        )

    def p_all(sem):
        ref = qbuf.at[pl.ds(0, N_CTX - 1)]
        return pltpu.make_async_copy(ref, ref, sem)

    @pl.loop(1, N_CTX)
    def _(i):
        p_copy(i).start()

    qbuf[c] = pbuf[core, pair]
    out_gq = pltpu.make_async_copy(gq_ref, gq_hbm, out_sem.at[0])
    out_gq.start()

    b_shared().wait()
    for blk in range(2):
        chosen = bcols[bt_ref[blk]]
        padded = jnp.concatenate([chosen, jnp.zeros_like(chosen)], axis=0)
        part = nt_dot(gq[blk * HD : (blk + 1) * HD, :], padded) * 2.0
        rsend[pl.ds(blk * 8, 8)] = part.reshape(8, 16, HD)

    def r_copy(i):
        to = (a + i) % N_ADP
        return pltpu.make_async_remote_copy(
            src_ref=rsend.at[to], dst_ref=rbuf.at[a], send_sem=r_send, recv_sem=r_recv,
            device_id={"ctx": c, "adp": to}, device_id_type=MESH,
        )

    def r_all(sem):
        ref = rbuf.at[pl.ds(0, N_ADP - 1)]
        return pltpu.make_async_copy(ref, ref, sem)

    @pl.loop(1, N_ADP)
    def _(i):
        r_copy(i).start()

    rbuf[a] = rsend[a]

    bt_all(bt_recv).wait()
    bt_all(bt_send).wait()
    b_all(b_send).wait()
    b_share().wait_send()
    along(c, plus_send, z_plus).wait_send()
    along(c, minus_send, z_minus).wait_send()
    along(c, sib_send, sib).wait_send()
    rest_to_sib(c).wait_send()

    @pl.when(y_hi == 0)
    def _():
        to_y().wait_send()

    @pl.loop(4, 24)
    def _(e):
        valid, src_pair, on_plus, on_minus = event(e)
        chunk = src_pair * 2 + core

        @pl.when(on_plus)
        def _():
            along(chunk, plus_send, z_plus).wait_send()

        @pl.when(on_minus)
        def _():
            along(chunk, minus_send, z_minus).wait_send()

        @pl.when(valid)
        def _():
            await_swap_sent(chunk)
            along(chunk, sib_send, sib).wait_send()
            rest_to_sib(chunk).wait_send()

    p_all(p_recv).wait()
    upper = lax.broadcasted_iota(jnp.int32, (8, HD), 0) < 4

    def add_source(i, sums):
        tile = qbuf[i]
        owner = jnp.where(
            upper, jnp.broadcast_to(btile[i, 0:1, :], (8, HD)), jnp.broadcast_to(btile[i, 1:2, :], (8, HD))
        )
        return tuple(s + jnp.where(owner == t, tile, 0.0) for t, s in enumerate(sums))

    sums = lax.fori_loop(0, N_CTX, add_source, tuple(jnp.zeros((8, HD), F32) for _ in range(N_ADP)))
    for t in range(N_ADP):
        tbuf[t] = sums[t]

    def g_copy(t):
        return pltpu.make_async_remote_copy(
            src_ref=tbuf.at[t], dst_ref=gbuf.at[pair], send_sem=g_send, recv_sem=g_recv,
            device_id={"ctx": a * 2 + core, "adp": t}, device_id_type=MESH,
        )

    def g_wait(sem):
        @pl.when(selfdest == 0)
        def _():
            pltpu.make_async_copy(gbuf, gbuf, sem).wait()

        @pl.when(selfdest == 1)
        def _():
            ref = gbuf.at[pl.ds(0, N_ADP - 1)]
            pltpu.make_async_copy(ref, ref, sem).wait()

    @pl.loop(0, N_ADP)
    def _(i):
        t = (a + i) % N_ADP

        @pl.when(jnp.logical_not((pair == a) & (t == a)))
        def _():
            g_copy(t).start()

    @pl.when(pair == a)
    def _():
        gbuf[pair] = tbuf[a]

    r_all(r_recv).wait()
    share = rbuf[0]
    for i in range(1, N_ADP):
        share = share + rbuf[i]
    glr_ref[...] = share[:, :RANK]
    out_glr = pltpu.make_async_copy(glr_ref, glr_hbm, out_sem.at[1])
    out_glr.start()
    p_all(p_send).wait()
    r_all(r_send).wait()
    out_gq.wait()

    g_wait(g_recv)
    for i in range(N_ADP):
        tile = gbuf[i]
        ga_ref[0, pl.ds(i * 4, 4), :] = tile[0:4] + tile[4:8]
    out_ga = pltpu.make_async_copy(ga_ref, ga_hbm, out_sem.at[2])
    out_ga.start()
    g_wait(g_send)
    out_glr.wait()
    out_ga.wait()


def on_device(queries, keys, values, grad_out, docs, block_tenant, low_rank, adapter_b):
    anywhere = pl.BlockSpec(memory_space=pl.ANY)
    dma = pltpu.SemaphoreType.DMA
    return pl.pallas_call(
        body,
        out_shape=(
            jax.ShapeDtypeStruct((TOK, 2 * HD), BF16),
            jax.ShapeDtypeStruct((16, RANK), F32),
            jax.ShapeDtypeStruct((1, RANK, HD), F32),
        ),
        in_specs=[anywhere] * 8,
        out_specs=(anywhere,) * 3,
        scratch_shapes=[
            pltpu.VMEM((N_CTX, 2, SLOT, HD), BF16),
            pltpu.VMEM((SLOT, HD), BF16),
            pltpu.VMEM((TOK, 2 * HD), BF16),
            pltpu.VMEM((TOK, 2 * HD), BF16),
            pltpu.VMEM((2, HD), jnp.int32),
            pltpu.SMEM((2,), jnp.int32),
            pltpu.VMEM((RANK, TOK), BF16),
            pltpu.VMEM((TOK, 2 * HD), BF16),
            pltpu.VMEM((16, RANK), F32),
            pltpu.VMEM((1, RANK, HD), F32),
            pltpu.VMEM((2, 2 * TOK, 2 * HD), F32),
            pltpu.VMEM((2, TOK, HD), F32),
            pltpu.VMEM((TOK, HD), F32),
            pltpu.VMEM((N_ADP, RANK, 2 * HD), BF16),
            pltpu.VMEM((N_CTX, 2, HD), jnp.int32),
            pltpu.VMEM((2 * RANK, TOK), BF16),
            pltpu.VMEM((2, N_ADP, 8, HD), F32),
            pltpu.VMEM((N_CTX, 8, HD), F32),
            pltpu.VMEM((N_ADP, 8, HD), F32),
            pltpu.VMEM((N_ADP, 8, HD), F32),
            pltpu.VMEM((N_ADP, 16, HD), F32),
            pltpu.VMEM((N_ADP, 16, HD), F32),
            dma((9,)), dma((N_CTX,)), dma((N_CTX,)), dma((N_CTX,)), dma((N_CTX,)),
            dma((N_CTX,)), dma((N_CTX,)), dma((N_CTX,)), dma,
            dma, dma, dma, dma, dma, dma, dma, dma, dma, dma, dma, dma, dma((3,)),
        ],
        compiler_params=pltpu.CompilerParams(
            collective_id=0, has_side_effects=True, vmem_limit_bytes=60 * 1024 * 1024
        ),
        cost_estimate=pl.CostEstimate(flops=4_000_000_000, bytes_accessed=4_000_000, transcendentals=4_000_000),
    )(
        queries, keys, values, grad_out, docs.reshape(2, HD), block_tenant, low_rank.T, adapter_b
    )


def solution(mesh):
    placed = (
        P("ctx", "adp"),
        P("ctx", None),
        P("ctx", None),
        P("ctx", "adp"),
        P("ctx"),
        P("ctx"),
        P("ctx", None),
        P("adp", None, None),
    )
    return jax.shard_map(
        on_device,
        mesh=mesh,
        in_specs=placed,
        out_specs=(P("ctx", "adp"), P(("ctx", "adp"), None), P("adp", None, "ctx")),
        check_vma=False,
    )
```

```python
import math

import jax
import jax.numpy as jnp
from jax import lax
from jax.experimental import pallas as pl
from jax.experimental.pallas import tpu as pltpu
from jax.sharding import PartitionSpec as P

HD = 128
RANK = 64
TOK = 256
NZ = 8
NX = 4
NYL = 4
N_CTX = 32
N_ADP = 16
SLOT = TOK + 16
HALF = TOK // 2
EXP2_SCALE = HD ** (-0.5) * math.log2(math.e)
FAR = -1e30
MESH = pl.DeviceIdType.MESH
F32 = jnp.float32
BF16 = jnp.bfloat16


def rem(value, by):
    return lax.rem(value, jnp.int32(by))


def div(value, by):
    return lax.div(value, jnp.int32(by))


def nt_dot(a, b):
    return lax.dot_general(a, b, (((1,), (1,)), ((), ())), preferred_element_type=F32)


def body(
    q_hbm, k_hbm, v_hbm, go_hbm, docs_hbm, bt_hbm, low_hbm, b_hbm,
    gq_hbm, glr_hbm, ga_hbm,
    kv, xkv, q_ref, go_ref, docs_ref, bt_ref, low_ref, gq_ref, glr_ref, ga_ref,
    acc, row_top, qdoc, bcols, bt_mine, btile, lowt, pbuf, qbuf, tbuf, gbuf, rsend, rbuf,
    loc_sem, mine_recv, other_recv, plus_send, minus_send, sib_send, sib2_send, x_send, y_send,
    bt_recv, bt_send, b_recv, b_send, bs_recv, bs_send,
    r_recv, r_send, p_recv, p_send, g_recv, g_send, out_sem,
):
    c = lax.axis_index("ctx")
    a = lax.axis_index("adp")
    core = rem(c, 2)
    pair = div(c, 2)
    z = rem(pair, NZ)
    y_hi = div(pair, NZ)
    head = div(a, NX)
    x = rem(a, NX)
    mine = rem(x, 2)
    other = 1 - mine
    sib = pair * 2 + (1 - core)
    z_plus = (y_hi * NZ + rem(z + 1, NZ)) * 2 + core
    z_minus = (y_hi * NZ + rem(z + NZ - 1, NZ)) * 2 + core
    x_plus = head * NX + rem(x + 1, NX)
    x_minus = head * NX + rem(x + NX - 1, NX)
    y_ctx = ((1 - y_hi) * NZ + z) * 2 + core
    y_adp = (NYL - 1 - head) * NX + x
    selfdest = (pair == a).astype(jnp.int32)

    barrier = pltpu.get_barrier_semaphore()

    def greet(ctx, adp):
        pl.semaphore_signal(barrier, inc=1, device_id={"ctx": ctx, "adp": adp}, device_id_type=MESH)

    greet(y_ctx, y_adp)
    greet(z_plus, a)
    greet(z_minus, a)
    greet(sib, a)

    @pl.loop(1, N_ADP)
    def _(i):
        greet(c, rem(a + i, N_ADP))

    @pl.loop(0, N_CTX)
    def _(i):
        @pl.when(jnp.logical_not((pair == a) & (i == c)))
        def _():
            greet(i, pair)

    def col(which):
        return pl.ds(pl.multiple_of(which * HD, HD), HD)

    far_head = NYL - 1 - head
    get_docs = pltpu.make_async_copy(docs_hbm, docs_ref, loc_sem.at[0])
    own_k = pltpu.make_async_copy(k_hbm.at[:, col(head)], kv.at[c, 0, pl.ds(0, TOK)], loc_sem.at[1])
    own_v = pltpu.make_async_copy(v_hbm.at[:, col(head)], kv.at[c, 1, pl.ds(0, TOK)], loc_sem.at[2])
    x_k = pltpu.make_async_copy(k_hbm.at[:, col(far_head)], xkv.at[pl.ds(0, TOK)], loc_sem.at[3])
    x_v = pltpu.make_async_copy(v_hbm.at[:, col(far_head)], xkv.at[pl.ds(0, TOK)], loc_sem.at[3])
    get_q = pltpu.make_async_copy(q_hbm, q_ref, loc_sem.at[4])
    get_go = pltpu.make_async_copy(go_hbm, go_ref, loc_sem.at[5])
    get_bt = pltpu.make_async_copy(bt_hbm, bt_ref, loc_sem.at[6])
    get_low = pltpu.make_async_copy(low_hbm, low_ref, loc_sem.at[7])
    half = pl.multiple_of(core * (RANK // 2), RANK // 2)
    own_b = pltpu.make_async_copy(
        b_hbm.at[0, pl.ds(half, RANK // 2), pl.ds(pl.multiple_of(a * 2 * HD, 2 * HD), 2 * HD)],
        bcols.at[a, pl.ds(half, RANK // 2)],
        loc_sem.at[8],
    )
    get_docs.start()
    own_k.start()
    own_v.start()

    @pl.when(mine == 0)
    def _():
        x_k.start()

    @pl.when(mine == 1)
    def _():
        x_v.start()

    get_bt.start()
    get_q.start()
    get_go.start()
    get_low.start()
    own_b.start()

    get_docs.wait()
    doc_rows = docs_ref[...].astype(F32)
    tag = jnp.concatenate([doc_rows, jnp.zeros((14, HD), F32)], axis=0).astype(BF16)
    kv[c, mine, pl.ds(TOK, 16), :] = tag
    xkv[pl.ds(TOK, 16), :] = tag
    own_k.wait()
    own_v.wait()
    x_k.wait()
    pl.semaphore_wait(barrier, 4 + (N_ADP - 1) + N_CTX - selfdest)

    def along(chunk, send_sem, to):
        ref = kv.at[chunk, mine]
        return pltpu.make_async_remote_copy(
            src_ref=ref, dst_ref=ref, send_sem=send_sem.at[chunk], recv_sem=mine_recv.at[chunk],
            device_id={"ctx": to, "adp": a}, device_id_type=MESH,
        )

    def rest_to_sib(chunk):
        ref = kv.at[chunk, other, pl.ds(0, TOK)]
        return pltpu.make_async_remote_copy(
            src_ref=ref, dst_ref=ref, send_sem=sib2_send.at[chunk], recv_sem=other_recv.at[chunk],
            device_id={"ctx": sib, "adp": a}, device_id_type=MESH,
        )

    def swap(chunk, first, to):
        ref = kv.at[chunk, mine, pl.ds(first, HALF)]
        return pltpu.make_async_remote_copy(
            src_ref=ref, dst_ref=ref, send_sem=x_send.at[chunk], recv_sem=other_recv.at[chunk],
            device_id={"ctx": c, "adp": to}, device_id_type=MESH,
        )

    def to_y():
        return pltpu.make_async_remote_copy(
            src_ref=xkv, dst_ref=kv.at[c, mine], send_sem=y_send, recv_sem=mine_recv.at[c],
            device_id={"ctx": y_ctx, "adp": y_adp}, device_id_type=MESH,
        )

    def await_mine(chunk):
        ref = kv.at[chunk, mine]
        pltpu.make_async_copy(ref, ref, mine_recv.at[chunk]).wait()

    def await_other(chunk):
        ref = kv.at[chunk, other, pl.ds(0, TOK)]
        pltpu.make_async_copy(ref, ref, other_recv.at[chunk]).wait()

    def await_swap_sent(chunk):
        ref = kv.at[chunk, mine, pl.ds(0, TOK)]
        pltpu.make_async_copy(ref, ref, x_send.at[chunk]).wait()

    along(c, plus_send, z_plus).start()
    along(c, minus_send, z_minus).start()

    @pl.when(y_hi == 0)
    def _():
        to_y().start()

    along(c, sib_send, sib).start()
    rest_to_sib(c).start()

    def b_copy(i):
        to = rem(a + i, N_ADP)
        return pltpu.make_async_remote_copy(
            src_ref=b_hbm.at[0, pl.ds(half, RANK // 2), pl.ds(pl.multiple_of(to * 2 * HD, 2 * HD), 2 * HD)],
            dst_ref=bcols.at[a, pl.ds(half, RANK // 2)],
            send_sem=b_send, recv_sem=b_recv,
            device_id={"ctx": c, "adp": to}, device_id_type=MESH,
        )

    def b_all(sem):
        ref = bcols.at[pl.ds(0, N_ADP - 1), pl.ds(half, RANK // 2)]
        return pltpu.make_async_copy(ref, ref, sem)

    def b_share():
        ref = bcols.at[:, pl.ds(half, RANK // 2)]
        return pltpu.make_async_remote_copy(
            src_ref=ref, dst_ref=ref, send_sem=bs_send, recv_sem=bs_recv,
            device_id={"ctx": sib, "adp": a}, device_id_type=MESH,
        )

    def b_shared():
        ref = bcols.at[:, pl.ds(pl.multiple_of((1 - core) * (RANK // 2), RANK // 2), RANK // 2)]
        return pltpu.make_async_copy(ref, ref, bs_recv)

    @pl.loop(1, N_ADP)
    def _(i):
        b_copy(i).start()

    get_bt.wait()
    bt_mine[...] = jnp.where(lax.broadcasted_iota(jnp.int32, (2, HD), 0) == 0, bt_ref[0], bt_ref[1])

    def to_sum(i):
        return a * 2 + rem(i, 2), rem(a + div(i, 2), N_ADP)

    def bt_copy(i):
        ctx, adp = to_sum(i)
        return pltpu.make_async_remote_copy(
            src_ref=bt_mine, dst_ref=btile.at[c], send_sem=bt_send, recv_sem=bt_recv,
            device_id={"ctx": ctx, "adp": adp}, device_id_type=MESH,
        )

    def wait_all(buffer, sem):
        @pl.when(selfdest == 0)
        def _():
            pltpu.make_async_copy(buffer, buffer, sem).wait()

        @pl.when(selfdest == 1)
        def _():
            ref = buffer.at[pl.ds(0, N_CTX - 1)]
            pltpu.make_async_copy(ref, ref, sem).wait()

    def is_self(i):
        return (selfdest == 1) & (i == core)

    @pl.loop(0, N_CTX)
    def _(i):
        @pl.when(jnp.logical_not(is_self(i)))
        def _():
            bt_copy(i).start()

    @pl.when(selfdest == 1)
    def _():
        btile[c] = bt_mine[...]

    get_low.wait()
    rr = lax.broadcasted_iota(jnp.int32, (2 * RANK, RANK), 0)
    kk = lax.broadcasted_iota(jnp.int32, (2 * RANK, RANK), 1)
    pick = jnp.where(kk == ((rr >> 3) * 4 + (rr & 3)), 1.0, 0.0).astype(BF16)
    spread = jnp.dot(pick, low_ref[...], preferred_element_type=F32)
    rr = lax.broadcasted_iota(jnp.int32, (2 * RANK, TOK), 0)
    tt = lax.broadcasted_iota(jnp.int32, (2 * RANK, TOK), 1)
    lowt[...] = jnp.where((tt >> 7) == ((rr >> 2) & 1), spread, 0.0).astype(BF16)

    ri = lax.broadcasted_iota(jnp.int32, (HD, HD), 0)
    ci = lax.broadcasted_iota(jnp.int32, (HD, HD), 1)
    for part in range(2):
        spot = jnp.where(ri == ci, jnp.broadcast_to(doc_rows[part : part + 1, :], (HD, HD)), 0.0)
        column = jnp.sum(spot, axis=1, keepdims=True)
        qdoc[pl.ds(part * HD, HD), :] = jnp.broadcast_to(column, (HD, HD))

    ones = jnp.ones((TOK, HD), BF16)

    def attend(which, first):
        low_slot = which * 2
        row_doc = qdoc[...]
        for h in range(2):
            q_h = q_ref[:, h * HD : (h + 1) * HD]
            g_h = go_ref[:, h * HD : (h + 1) * HD]
            tiles = []
            for half_pair in range(2):
                scores = nt_dot(q_h, kv[low_slot + half_pair, 0, pl.ds(0, TOK), :])
                key_doc = kv[low_slot + half_pair, mine, pl.ds(TOK, 16), :].astype(F32)
                for lt in range(2):
                    seen = row_doc == key_doc[lt : lt + 1, :]
                    if first:
                        rpos = lax.broadcasted_iota(jnp.int32, (TOK, HD), 0) + core * TOK
                        kpos = lax.broadcasted_iota(jnp.int32, (TOK, HD), 1) + (half_pair * TOK + lt * HD)
                        seen = seen & (kpos <= rpos)
                    tiles.append(jnp.where(seen, scores[:, lt * HD : (lt + 1) * HD], FAR))
            top = jnp.maximum(jnp.maximum(tiles[0], tiles[1]), jnp.maximum(tiles[2], tiles[3]))
            top = jnp.broadcast_to(jnp.max(top, axis=1, keepdims=True), (TOK, HD))
            if not first:
                before = row_top[h]
                top = jnp.maximum(top, before)
                decay = jnp.exp2((before - top) * EXP2_SCALE)
            row_top[h] = top
            total = None
            for half_pair in range(2):
                weights = [
                    jnp.exp2((tiles[half_pair * 2 + lt] - top) * EXP2_SCALE) for lt in range(2)
                ]
                weights = jnp.concatenate(weights, axis=1)
                gw = nt_dot(g_h, kv[low_slot + half_pair, 1, pl.ds(0, TOK), :])
                both = jnp.concatenate([weights.astype(BF16), (weights * gw).astype(BF16)], axis=0)
                right = jnp.concatenate([kv[low_slot + half_pair, 0, pl.ds(0, TOK), :], ones], axis=1)
                term = jnp.dot(both, right, preferred_element_type=F32)
                total = term if total is None else total + term
            if first:
                acc[h] = total
            else:
                wide = jnp.concatenate([decay, decay], axis=1)
                wide = jnp.concatenate([wide, wide], axis=0)
                acc[h] = acc[h] * wide + total

    get_q.wait()
    get_go.wait()
    await_mine(sib)
    await_other(sib)
    attend(pair, True)

    def event(e):
        late = e >= 4
        e = jnp.maximum(e, 0)
        s, u = div(e, 4), rem(e, 4)
        lower, back = div(u, 2), rem(u, 2)
        dist = s - lower
        valid = late & (dist >= 0) & (lower <= y_hi)
        valid = valid & ((dist > 0) | ((lower == 1) & (back == 0)))
        valid = valid & ((dist <= 3) | ((dist == 4) & (back != lower)))
        from_z = rem(z + NZ + dist * (2 * back - 1), NZ)
        src_pair = (y_hi - y_hi * lower) * NZ + from_z
        on_plus = valid & ((back == 0) | (dist == 0)) & ((dist <= 2) | ((dist == 3) & (lower == 1)))
        on_minus = valid & ((back == 1) | (dist == 0)) & ((dist <= 2) | ((dist == 3) & (lower == 0)))
        return valid, src_pair, on_plus, on_minus

    @pl.loop(4, 28)
    def _(e):
        valid, src_pair, on_plus, on_minus = event(e)
        chunk = src_pair * 2 + core

        @pl.when(valid)
        def _():
            await_mine(chunk)

            @pl.when(on_plus)
            def _():
                along(chunk, plus_send, z_plus).start()

            @pl.when(on_minus)
            def _():
                along(chunk, minus_send, z_minus).start()

            swap(chunk, 0, x_plus).start()
            swap(chunk, HALF, x_minus).start()
            along(chunk, sib_send, sib).start()

        ready, src_pair, _, _ = event(e - 3)
        chunk2 = src_pair * 2 + core

        @pl.when(ready)
        def _():
            await_other(chunk2)
            rest_to_sib(chunk2).start()

        whole, last_pair, _, _ = event(e - 5)

        @pl.when(whole)
        def _():
            await_mine(last_pair * 2 + 1 - core)
            await_other(last_pair * 2 + 1 - core)

        @pl.when(whole & (last_pair < pair))
        def _():
            attend(last_pair, False)

    b_all(b_recv).wait()
    own_b.wait()
    b_share().start()

    for h in range(2):
        total = acc[h, pl.ds(0, TOK), pl.ds(HD, HD)]
        inv = 1.0 / total
        delta = acc[h, pl.ds(TOK, TOK), pl.ds(HD, HD)] * inv
        grad = (acc[h, pl.ds(TOK, TOK), pl.ds(0, HD)] - delta * acc[h, pl.ds(0, TOK), pl.ds(0, HD)]) * inv
        gq_ref[:, h * HD : (h + 1) * HD] = (grad * HD ** (-0.5)).astype(BF16)

    gq = gq_ref[...]
    partial = jnp.dot(lowt[...], gq, preferred_element_type=F32) * 2.0
    for h in range(2):
        pbuf[h] = partial[:, h * HD : (h + 1) * HD].reshape(N_ADP, 8, HD)

    def p_copy(i):
        ctx, adp = to_sum(i)
        return pltpu.make_async_remote_copy(
            src_ref=pbuf.at[rem(i, 2), adp], dst_ref=qbuf.at[c],
            send_sem=p_send, recv_sem=p_recv,
            device_id={"ctx": ctx, "adp": adp}, device_id_type=MESH,
        )

    @pl.loop(0, N_CTX)
    def _(i):
        @pl.when(jnp.logical_not(is_self(i)))
        def _():
            p_copy(i).start()

    @pl.when(selfdest == 1)
    def _():
        qbuf[c] = pbuf[core, a]

    out_gq = pltpu.make_async_copy(gq_ref, gq_hbm, out_sem.at[0])
    out_gq.start()

    b_shared().wait()
    for blk in range(2):
        chosen = bcols[bt_ref[blk]]
        padded = jnp.concatenate([chosen, jnp.zeros_like(chosen)], axis=0)
        part = nt_dot(gq[blk * HD : (blk + 1) * HD, :], padded) * 2.0
        rsend[pl.ds(blk * 8, 8)] = part.reshape(8, 16, HD)

    def r_copy(i):
        to = rem(a + i, N_ADP)
        return pltpu.make_async_remote_copy(
            src_ref=rsend.at[to], dst_ref=rbuf.at[a], send_sem=r_send, recv_sem=r_recv,
            device_id={"ctx": c, "adp": to}, device_id_type=MESH,
        )

    def r_all(sem):
        ref = rbuf.at[pl.ds(0, N_ADP - 1)]
        return pltpu.make_async_copy(ref, ref, sem)

    @pl.loop(1, N_ADP)
    def _(i):
        r_copy(i).start()

    rbuf[a] = rsend[a]

    wait_all(btile, bt_recv)
    wait_all(btile, bt_send)
    b_all(b_send).wait()
    b_share().wait_send()
    along(c, plus_send, z_plus).wait_send()
    along(c, minus_send, z_minus).wait_send()
    along(c, sib_send, sib).wait_send()
    rest_to_sib(c).wait_send()

    @pl.when(y_hi == 0)
    def _():
        to_y().wait_send()

    @pl.loop(4, 24)
    def _(e):
        valid, src_pair, on_plus, on_minus = event(e)
        chunk = src_pair * 2 + core

        @pl.when(on_plus)
        def _():
            along(chunk, plus_send, z_plus).wait_send()

        @pl.when(on_minus)
        def _():
            along(chunk, minus_send, z_minus).wait_send()

        @pl.when(valid)
        def _():
            await_swap_sent(chunk)
            along(chunk, sib_send, sib).wait_send()
            rest_to_sib(chunk).wait_send()

    wait_all(qbuf, p_recv)
    upper = lax.broadcasted_iota(jnp.int32, (8, HD), 0) < 4

    def add_source(i, sums):
        tile = qbuf[i]
        owner = jnp.where(
            upper, jnp.broadcast_to(btile[i, 0:1, :], (8, HD)), jnp.broadcast_to(btile[i, 1:2, :], (8, HD))
        )
        return tuple(s + jnp.where(owner == t, tile, 0.0) for t, s in enumerate(sums))

    sums = lax.fori_loop(0, N_CTX, add_source, tuple(jnp.zeros((8, HD), F32) for _ in range(N_ADP)))
    for t in range(N_ADP):
        tbuf[t] = sums[t]

    def g_copy(i):
        to = rem(a + i, N_ADP)
        return pltpu.make_async_remote_copy(
            src_ref=tbuf.at[to], dst_ref=gbuf.at[a], send_sem=g_send, recv_sem=g_recv,
            device_id={"ctx": c, "adp": to}, device_id_type=MESH,
        )

    def g_all(sem):
        ref = gbuf.at[pl.ds(0, N_ADP - 1)]
        return pltpu.make_async_copy(ref, ref, sem)

    @pl.loop(1, N_ADP)
    def _(i):
        g_copy(i).start()

    gbuf[a] = tbuf[a]

    r_all(r_recv).wait()
    share = rbuf[0]
    for i in range(1, N_ADP):
        share = share + rbuf[i]
    glr_ref[...] = share[:, :RANK]
    out_glr = pltpu.make_async_copy(glr_ref, glr_hbm, out_sem.at[1])
    out_glr.start()
    wait_all(qbuf, p_send)
    r_all(r_send).wait()
    out_gq.wait()

    g_all(g_recv).wait()
    for i in range(N_ADP):
        tile = gbuf[i]
        ga_ref[0, pl.ds(i * 4, 4), :] = tile[0:4] + tile[4:8]
    out_ga = pltpu.make_async_copy(ga_ref, ga_hbm, out_sem.at[2])
    out_ga.start()
    g_all(g_send).wait()
    out_glr.wait()
    out_ga.wait()


def finish(gq_in, glr_in, ga_in, gq_out, glr_out, ga_out, sems):
    copies = [
        pltpu.make_async_copy(gq_in, gq_out, sems.at[0]),
        pltpu.make_async_copy(glr_in, glr_out, sems.at[1]),
        pltpu.make_async_copy(ga_in, ga_out, sems.at[2]),
    ]
    for copy in copies:
        copy.start()
    for copy in copies:
        copy.wait()


def on_device(queries, keys, values, grad_out, docs, block_tenant, low_rank, adapter_b):
    anywhere = pl.BlockSpec(memory_space=pl.ANY)
    dma = pltpu.SemaphoreType.DMA
    shapes = (
        jax.ShapeDtypeStruct((TOK, 2 * HD), BF16),
        jax.ShapeDtypeStruct((16, RANK), F32),
        jax.ShapeDtypeStruct((1, RANK, HD), F32),
    )
    grads = pl.pallas_call(
        body,
        out_shape=shapes,
        in_specs=[anywhere] * 8,
        out_specs=(anywhere,) * 3,
        scratch_shapes=[
            pltpu.VMEM((N_CTX, 2, SLOT, HD), BF16),
            pltpu.VMEM((SLOT, HD), BF16),
            pltpu.VMEM((TOK, 2 * HD), BF16),
            pltpu.VMEM((TOK, 2 * HD), BF16),
            pltpu.VMEM((2, HD), jnp.int32),
            pltpu.SMEM((2,), jnp.int32),
            pltpu.VMEM((RANK, TOK), BF16),
            pltpu.VMEM((TOK, 2 * HD), BF16),
            pltpu.VMEM((16, RANK), F32),
            pltpu.VMEM((1, RANK, HD), F32),
            pltpu.VMEM((2, 2 * TOK, 2 * HD), F32),
            pltpu.VMEM((2, TOK, HD), F32),
            pltpu.VMEM((TOK, HD), F32),
            pltpu.VMEM((N_ADP, RANK, 2 * HD), BF16),
            pltpu.VMEM((2, HD), jnp.int32),
            pltpu.VMEM((N_CTX, 2, HD), jnp.int32),
            pltpu.VMEM((2 * RANK, TOK), BF16),
            pltpu.VMEM((2, N_ADP, 8, HD), F32),
            pltpu.VMEM((N_CTX, 8, HD), F32),
            pltpu.VMEM((N_ADP, 8, HD), F32),
            pltpu.VMEM((N_ADP, 8, HD), F32),
            pltpu.VMEM((N_ADP, 16, HD), F32),
            pltpu.VMEM((N_ADP, 16, HD), F32),
            dma((9,)), dma((N_CTX,)), dma((N_CTX,)), dma((N_CTX,)), dma((N_CTX,)),
            dma((N_CTX,)), dma((N_CTX,)), dma((N_CTX,)), dma,
            dma, dma, dma, dma, dma, dma, dma, dma, dma, dma, dma, dma, dma((3,)),
        ],
        compiler_params=pltpu.CompilerParams(
            collective_id=0, has_side_effects=True, vmem_limit_bytes=60 * 1024 * 1024
        ),
        cost_estimate=pl.CostEstimate(flops=4_000_000_000, bytes_accessed=4_000_000, transcendentals=4_000_000),
    )(
        queries, keys, values, grad_out, docs.reshape(2, HD), block_tenant, low_rank.T, adapter_b
    )
    return pl.pallas_call(
        finish,
        out_shape=shapes,
        in_specs=[anywhere] * 3,
        out_specs=(anywhere,) * 3,
        scratch_shapes=[dma((3,))],
        compiler_params=pltpu.CompilerParams(vmem_limit_bytes=60 * 1024 * 1024),
    )(*grads)


def solution(mesh):
    placed = (
        P("ctx", "adp"),
        P("ctx", None),
        P("ctx", None),
        P("ctx", "adp"),
        P("ctx"),
        P("ctx"),
        P("ctx", None),
        P("adp", None, None),
    )
    return jax.shard_map(
        on_device,
        mesh=mesh,
        in_specs=placed,
        out_specs=(P("ctx", "adp"), P(("ctx", "adp"), None), P("adp", None, "ctx")),
        check_vma=False,
    )
```

```python
import math

import jax
import jax.numpy as jnp
from jax import lax
from jax.experimental import pallas as pl
from jax.experimental.pallas import tpu as pltpu
from jax.sharding import PartitionSpec as P

HD = 128
RANK = 64
TOK = 256
NZ = 8
NX = 4
NYL = 4
N_CTX = 32
N_ADP = 16
SLOT = TOK + 16
HALF = TOK // 2
EXP2_SCALE = HD ** (-0.5) * math.log2(math.e)
FAR = -1e30
MESH = pl.DeviceIdType.MESH
ARRIVALS = (1, 7, 3, 5, 8 + 0, 8 + 3, 8 + 5, 2, 6, 4, 8 + 1, 8 + 7, 8 + 2, 8 + 6, 8 + 4)
EARLY = sum(code << (4 * i) for i, code in enumerate(ARRIVALS[:7]))
LATE = sum(code << (4 * i) for i, code in enumerate(ARRIVALS[7:14]))
LAST = ARRIVALS[14]
LAG_SWAP, LAG_USE = 3, 5
F32 = jnp.float32
BF16 = jnp.bfloat16


def rem(value, by):
    return lax.rem(value, jnp.int32(by))


def div(value, by):
    return lax.div(value, jnp.int32(by))


def nt_dot(a, b):
    return lax.dot_general(a, b, (((1,), (1,)), ((), ())), preferred_element_type=F32)


def body(
    q_hbm, k_hbm, v_hbm, go_hbm, docs_hbm, bt_hbm, low_hbm, b_hbm,
    gq_hbm, glr_hbm, ga_hbm,
    kv, xkv, q_ref, go_ref, docs_ref, bt_ref, low_ref, gq_ref, glr_ref, ga_ref,
    acc, row_top, qdoc, bcols, bt_mine, btile, lowt, pbuf, qbuf, tbuf, gbuf, rsend, rbuf,
    loc_sem, mine_recv, other_recv, plus_send, minus_send, sib_send, sib2_send, x_send, y_send, far_send,
    bt_recv, bt_send, b_recv, b_send, bs_recv, bs_send,
    r_recv, r_send, p_recv, p_send, g_recv, g_send, out_sem,
):
    c = lax.axis_index("ctx")
    a = lax.axis_index("adp")
    core = rem(c, 2)
    pair = div(c, 2)
    z = rem(pair, NZ)
    y_hi = div(pair, NZ)
    head = div(a, NX)
    x = rem(a, NX)
    mine = rem(x, 2)
    other = 1 - mine
    sib = pair * 2 + (1 - core)
    z_plus = (y_hi * NZ + rem(z + 1, NZ)) * 2 + core
    z_minus = (y_hi * NZ + rem(z + NZ - 1, NZ)) * 2 + core
    z_plus3 = (y_hi * NZ + rem(z + 3, NZ)) * 2 + core
    z_minus3 = (y_hi * NZ + rem(z + NZ - 3, NZ)) * 2 + core
    x_plus = head * NX + rem(x + 1, NX)
    x_minus = head * NX + rem(x + NX - 1, NX)

    def y_ctx(step):
        return ((1 - y_hi) * NZ + rem(z + NZ + step, NZ)) * 2 + core

    y_adp = (NYL - 1 - head) * NX + x
    selfdest = (pair == a).astype(jnp.int32)

    barrier = pltpu.get_barrier_semaphore()

    def greet(ctx, adp):
        pl.semaphore_signal(barrier, inc=1, device_id={"ctx": ctx, "adp": adp}, device_id_type=MESH)

    greet(z_plus, a)
    greet(z_minus, a)
    greet(z_plus3, a)
    greet(z_minus3, a)
    greet(sib, a)

    @pl.when(y_hi == 1)
    def _():
        for step in (0, 3, -3):
            greet(y_ctx(step), y_adp)

    @pl.loop(1, N_ADP)
    def _(i):
        greet(c, rem(a + i, N_ADP))

    @pl.loop(0, N_CTX)
    def _(i):
        @pl.when(jnp.logical_not((pair == a) & (i == c)))
        def _():
            greet(i, pair)

    def col(which):
        return pl.ds(pl.multiple_of(which * HD, HD), HD)

    far_head = NYL - 1 - head
    get_docs = pltpu.make_async_copy(docs_hbm, docs_ref, loc_sem.at[0])
    own_k = pltpu.make_async_copy(k_hbm.at[:, col(head)], kv.at[c, 0, pl.ds(0, TOK)], loc_sem.at[1])
    own_v = pltpu.make_async_copy(v_hbm.at[:, col(head)], kv.at[c, 1, pl.ds(0, TOK)], loc_sem.at[2])
    x_k = pltpu.make_async_copy(k_hbm.at[:, col(far_head)], xkv.at[pl.ds(0, TOK)], loc_sem.at[3])
    x_v = pltpu.make_async_copy(v_hbm.at[:, col(far_head)], xkv.at[pl.ds(0, TOK)], loc_sem.at[3])
    get_q = pltpu.make_async_copy(q_hbm, q_ref, loc_sem.at[4])
    get_go = pltpu.make_async_copy(go_hbm, go_ref, loc_sem.at[5])
    get_bt = pltpu.make_async_copy(bt_hbm, bt_ref, loc_sem.at[6])
    get_low = pltpu.make_async_copy(low_hbm, low_ref, loc_sem.at[7])
    half = pl.multiple_of(core * (RANK // 2), RANK // 2)
    own_b = pltpu.make_async_copy(
        b_hbm.at[0, pl.ds(half, RANK // 2), pl.ds(pl.multiple_of(a * 2 * HD, 2 * HD), 2 * HD)],
        bcols.at[a, pl.ds(half, RANK // 2)],
        loc_sem.at[8],
    )
    get_docs.start()
    own_k.start()
    own_v.start()

    @pl.when(mine == 0)
    def _():
        x_k.start()

    @pl.when(mine == 1)
    def _():
        x_v.start()

    get_bt.start()
    get_q.start()
    get_go.start()
    get_low.start()
    own_b.start()

    get_docs.wait()
    doc_rows = docs_ref[...].astype(F32)
    tag = jnp.concatenate([doc_rows, jnp.zeros((14, HD), F32)], axis=0).astype(BF16)
    kv[c, mine, pl.ds(TOK, 16), :] = tag
    xkv[pl.ds(TOK, 16), :] = tag
    own_k.wait()
    own_v.wait()
    x_k.wait()
    pl.semaphore_wait(barrier, 5 + 3 * (1 - y_hi) + (N_ADP - 1) + N_CTX - selfdest)

    def along(chunk, send_sem, to):
        ref = kv.at[chunk, mine]
        return pltpu.make_async_remote_copy(
            src_ref=ref, dst_ref=ref, send_sem=send_sem.at[chunk], recv_sem=mine_recv.at[chunk],
            device_id={"ctx": to, "adp": a}, device_id_type=MESH,
        )

    def rest_to_sib(chunk):
        ref = kv.at[chunk, other, pl.ds(0, TOK)]
        return pltpu.make_async_remote_copy(
            src_ref=ref, dst_ref=ref, send_sem=sib2_send.at[chunk], recv_sem=other_recv.at[chunk],
            device_id={"ctx": sib, "adp": a}, device_id_type=MESH,
        )

    def swap(chunk, first, to):
        ref = kv.at[chunk, mine, pl.ds(first, HALF)]
        return pltpu.make_async_remote_copy(
            src_ref=ref, dst_ref=ref, send_sem=x_send.at[chunk], recv_sem=other_recv.at[chunk],
            device_id={"ctx": c, "adp": to}, device_id_type=MESH,
        )

    def to_y(which):
        return pltpu.make_async_remote_copy(
            src_ref=xkv, dst_ref=kv.at[c, mine], send_sem=y_send.at[which], recv_sem=mine_recv.at[c],
            device_id={"ctx": y_ctx((0, 3, -3)[which]), "adp": y_adp}, device_id_type=MESH,
        )

    def far(which):
        ref = kv.at[c, mine]
        return pltpu.make_async_remote_copy(
            src_ref=ref, dst_ref=ref, send_sem=far_send.at[which], recv_sem=mine_recv.at[c],
            device_id={"ctx": (z_plus3, z_minus3)[which], "adp": a}, device_id_type=MESH,
        )

    def await_mine(chunk):
        ref = kv.at[chunk, mine]
        pltpu.make_async_copy(ref, ref, mine_recv.at[chunk]).wait()

    def await_other(chunk):
        ref = kv.at[chunk, other, pl.ds(0, TOK)]
        pltpu.make_async_copy(ref, ref, other_recv.at[chunk]).wait()

    def await_swap_sent(chunk):
        ref = kv.at[chunk, mine, pl.ds(0, TOK)]
        pltpu.make_async_copy(ref, ref, x_send.at[chunk]).wait()

    along(c, plus_send, z_plus).start()
    along(c, minus_send, z_minus).start()

    far(0).start()
    far(1).start()

    @pl.when(y_hi == 0)
    def _():
        for which in range(3):
            to_y(which).start()

    along(c, sib_send, sib).start()
    rest_to_sib(c).start()

    def b_copy(i):
        to = rem(a + i, N_ADP)
        return pltpu.make_async_remote_copy(
            src_ref=b_hbm.at[0, pl.ds(half, RANK // 2), pl.ds(pl.multiple_of(to * 2 * HD, 2 * HD), 2 * HD)],
            dst_ref=bcols.at[a, pl.ds(half, RANK // 2)],
            send_sem=b_send, recv_sem=b_recv,
            device_id={"ctx": c, "adp": to}, device_id_type=MESH,
        )

    def b_all(sem):
        ref = bcols.at[pl.ds(0, N_ADP - 1), pl.ds(half, RANK // 2)]
        return pltpu.make_async_copy(ref, ref, sem)

    def b_share():
        ref = bcols.at[:, pl.ds(half, RANK // 2)]
        return pltpu.make_async_remote_copy(
            src_ref=ref, dst_ref=ref, send_sem=bs_send, recv_sem=bs_recv,
            device_id={"ctx": sib, "adp": a}, device_id_type=MESH,
        )

    def b_shared():
        ref = bcols.at[:, pl.ds(pl.multiple_of((1 - core) * (RANK // 2), RANK // 2), RANK // 2)]
        return pltpu.make_async_copy(ref, ref, bs_recv)

    @pl.loop(1, N_ADP)
    def _(i):
        b_copy(i).start()

    get_bt.wait()
    bt_mine[...] = jnp.where(lax.broadcasted_iota(jnp.int32, (2, HD), 0) == 0, bt_ref[0], bt_ref[1])

    def to_sum(i):
        return a * 2 + rem(i, 2), rem(a + div(i, 2), N_ADP)

    def bt_copy(i):
        ctx, adp = to_sum(i)
        return pltpu.make_async_remote_copy(
            src_ref=bt_mine, dst_ref=btile.at[c], send_sem=bt_send, recv_sem=bt_recv,
            device_id={"ctx": ctx, "adp": adp}, device_id_type=MESH,
        )

    def wait_all(buffer, sem):
        @pl.when(selfdest == 0)
        def _():
            pltpu.make_async_copy(buffer, buffer, sem).wait()

        @pl.when(selfdest == 1)
        def _():
            ref = buffer.at[pl.ds(0, N_CTX - 1)]
            pltpu.make_async_copy(ref, ref, sem).wait()

    def is_self(i):
        return (selfdest == 1) & (i == core)

    @pl.loop(0, N_CTX)
    def _(i):
        @pl.when(jnp.logical_not(is_self(i)))
        def _():
            bt_copy(i).start()

    @pl.when(selfdest == 1)
    def _():
        btile[c] = bt_mine[...]

    get_low.wait()
    rr = lax.broadcasted_iota(jnp.int32, (2 * RANK, RANK), 0)
    kk = lax.broadcasted_iota(jnp.int32, (2 * RANK, RANK), 1)
    pick = jnp.where(kk == ((rr >> 3) * 4 + (rr & 3)), 1.0, 0.0).astype(BF16)
    spread = jnp.dot(pick, low_ref[...], preferred_element_type=F32)
    rr = lax.broadcasted_iota(jnp.int32, (2 * RANK, TOK), 0)
    tt = lax.broadcasted_iota(jnp.int32, (2 * RANK, TOK), 1)
    lowt[...] = jnp.where((tt >> 7) == ((rr >> 2) & 1), spread, 0.0).astype(BF16)

    ri = lax.broadcasted_iota(jnp.int32, (HD, HD), 0)
    ci = lax.broadcasted_iota(jnp.int32, (HD, HD), 1)
    for part in range(2):
        spot = jnp.where(ri == ci, jnp.broadcast_to(doc_rows[part : part + 1, :], (HD, HD)), 0.0)
        column = jnp.sum(spot, axis=1, keepdims=True)
        qdoc[pl.ds(part * HD, HD), :] = jnp.broadcast_to(column, (HD, HD))

    ones = jnp.ones((TOK, HD), BF16)

    def attend(which, first):
        low_slot = which * 2
        row_doc = qdoc[...]
        for h in range(2):
            q_h = q_ref[:, h * HD : (h + 1) * HD]
            g_h = go_ref[:, h * HD : (h + 1) * HD]
            tiles = []
            for half_pair in range(2):
                scores = nt_dot(q_h, kv[low_slot + half_pair, 0, pl.ds(0, TOK), :])
                key_doc = kv[low_slot + half_pair, mine, pl.ds(TOK, 16), :].astype(F32)
                for lt in range(2):
                    seen = row_doc == key_doc[lt : lt + 1, :]
                    if first:
                        rpos = lax.broadcasted_iota(jnp.int32, (TOK, HD), 0) + core * TOK
                        kpos = lax.broadcasted_iota(jnp.int32, (TOK, HD), 1) + (half_pair * TOK + lt * HD)
                        seen = seen & (kpos <= rpos)
                    tiles.append(jnp.where(seen, scores[:, lt * HD : (lt + 1) * HD], FAR))
            top = jnp.maximum(jnp.maximum(tiles[0], tiles[1]), jnp.maximum(tiles[2], tiles[3]))
            top = jnp.broadcast_to(jnp.max(top, axis=1, keepdims=True), (TOK, HD))
            if not first:
                before = row_top[h]
                top = jnp.maximum(top, before)
                decay = jnp.exp2((before - top) * EXP2_SCALE)
            row_top[h] = top
            total = None
            for half_pair in range(2):
                weights = [
                    jnp.exp2((tiles[half_pair * 2 + lt] - top) * EXP2_SCALE) for lt in range(2)
                ]
                weights = jnp.concatenate(weights, axis=1)
                gw = nt_dot(g_h, kv[low_slot + half_pair, 1, pl.ds(0, TOK), :])
                both = jnp.concatenate([weights.astype(BF16), (weights * gw).astype(BF16)], axis=0)
                right = jnp.concatenate([kv[low_slot + half_pair, 0, pl.ds(0, TOK), :], ones], axis=1)
                term = jnp.dot(both, right, preferred_element_type=F32)
                total = term if total is None else total + term
            if first:
                acc[h] = total
            else:
                wide = jnp.concatenate([decay, decay], axis=1)
                wide = jnp.concatenate([wide, wide], axis=0)
                acc[h] = acc[h] * wide + total

    get_q.wait()
    get_go.wait()
    await_mine(sib)
    await_other(sib)
    attend(pair, True)

    def event(e):
        e_low = jnp.clip(e, 0, 6)
        e_high = jnp.clip(e - 7, 0, 6)
        code = jnp.where(
            e < 7, lax.shift_right_logical(jnp.int32(EARLY), 4 * e_low),
            jnp.where(e < 14, lax.shift_right_logical(jnp.int32(LATE), 4 * e_high), LAST),
        )
        code = code & 15
        lower, off = div(code, 8), rem(code, 8)
        valid = (e >= 0) & (e < len(ARRIVALS)) & (lower <= y_hi)
        src_pair = (y_hi - lower) * NZ + rem(z + NZ - off, NZ)
        on_plus = valid & ((off == 0) | (off == 5) | ((off == 3) & (lower == 1)))
        on_minus = valid & ((off == 0) | (off == 3) | ((off == 5) & (lower == 0)))
        return valid, src_pair, on_plus, on_minus

    @pl.loop(0, len(ARRIVALS) + LAG_USE)
    def _(e):
        valid, src_pair, on_plus, on_minus = event(e)
        chunk = src_pair * 2 + core

        @pl.when(valid)
        def _():
            await_mine(chunk)

            @pl.when(on_plus)
            def _():
                along(chunk, plus_send, z_plus).start()

            @pl.when(on_minus)
            def _():
                along(chunk, minus_send, z_minus).start()

            swap(chunk, 0, x_plus).start()
            swap(chunk, HALF, x_minus).start()
            along(chunk, sib_send, sib).start()

        ready, src_pair, _, _ = event(e - LAG_SWAP)
        chunk2 = src_pair * 2 + core

        @pl.when(ready)
        def _():
            await_other(chunk2)
            rest_to_sib(chunk2).start()

        whole, last_pair, _, _ = event(e - LAG_USE)

        @pl.when(whole)
        def _():
            await_mine(last_pair * 2 + 1 - core)
            await_other(last_pair * 2 + 1 - core)

        @pl.when(whole & (last_pair < pair))
        def _():
            attend(last_pair, False)

    b_all(b_recv).wait()
    own_b.wait()
    b_share().start()

    for h in range(2):
        total = acc[h, pl.ds(0, TOK), pl.ds(HD, HD)]
        inv = 1.0 / total
        delta = acc[h, pl.ds(TOK, TOK), pl.ds(HD, HD)] * inv
        grad = (acc[h, pl.ds(TOK, TOK), pl.ds(0, HD)] - delta * acc[h, pl.ds(0, TOK), pl.ds(0, HD)]) * inv
        gq_ref[:, h * HD : (h + 1) * HD] = (grad * HD ** (-0.5)).astype(BF16)

    gq = gq_ref[...]
    partial = jnp.dot(lowt[...], gq, preferred_element_type=F32) * 2.0
    for h in range(2):
        pbuf[h] = partial[:, h * HD : (h + 1) * HD].reshape(N_ADP, 8, HD)

    def p_copy(i):
        ctx, adp = to_sum(i)
        return pltpu.make_async_remote_copy(
            src_ref=pbuf.at[rem(i, 2), adp], dst_ref=qbuf.at[c],
            send_sem=p_send, recv_sem=p_recv,
            device_id={"ctx": ctx, "adp": adp}, device_id_type=MESH,
        )

    @pl.loop(0, N_CTX)
    def _(i):
        @pl.when(jnp.logical_not(is_self(i)))
        def _():
            p_copy(i).start()

    @pl.when(selfdest == 1)
    def _():
        qbuf[c] = pbuf[core, a]

    out_gq = pltpu.make_async_copy(gq_ref, gq_hbm, out_sem.at[0])
    out_gq.start()

    b_shared().wait()
    for blk in range(2):
        chosen = bcols[bt_ref[blk]]
        padded = jnp.concatenate([chosen, jnp.zeros_like(chosen)], axis=0)
        part = nt_dot(gq[blk * HD : (blk + 1) * HD, :], padded) * 2.0
        rsend[pl.ds(blk * 8, 8)] = part.reshape(8, 16, HD)

    def r_copy(i):
        to = rem(a + i, N_ADP)
        return pltpu.make_async_remote_copy(
            src_ref=rsend.at[to], dst_ref=rbuf.at[a], send_sem=r_send, recv_sem=r_recv,
            device_id={"ctx": c, "adp": to}, device_id_type=MESH,
        )

    def r_all(sem):
        ref = rbuf.at[pl.ds(0, N_ADP - 1)]
        return pltpu.make_async_copy(ref, ref, sem)

    @pl.loop(1, N_ADP)
    def _(i):
        r_copy(i).start()

    rbuf[a] = rsend[a]

    wait_all(btile, bt_recv)
    wait_all(btile, bt_send)
    b_all(b_send).wait()
    b_share().wait_send()
    along(c, plus_send, z_plus).wait_send()
    along(c, minus_send, z_minus).wait_send()
    along(c, sib_send, sib).wait_send()
    rest_to_sib(c).wait_send()

    far(0).wait_send()
    far(1).wait_send()

    @pl.when(y_hi == 0)
    def _():
        for which in range(3):
            to_y(which).wait_send()

    @pl.loop(0, len(ARRIVALS))
    def _(e):
        valid, src_pair, on_plus, on_minus = event(e)
        chunk = src_pair * 2 + core

        @pl.when(on_plus)
        def _():
            along(chunk, plus_send, z_plus).wait_send()

        @pl.when(on_minus)
        def _():
            along(chunk, minus_send, z_minus).wait_send()

        @pl.when(valid)
        def _():
            await_swap_sent(chunk)
            along(chunk, sib_send, sib).wait_send()
            rest_to_sib(chunk).wait_send()

    wait_all(qbuf, p_recv)
    upper = lax.broadcasted_iota(jnp.int32, (8, HD), 0) < 4

    def add_source(i, sums):
        tile = qbuf[i]
        owner = jnp.where(
            upper, jnp.broadcast_to(btile[i, 0:1, :], (8, HD)), jnp.broadcast_to(btile[i, 1:2, :], (8, HD))
        )
        return tuple(s + jnp.where(owner == t, tile, 0.0) for t, s in enumerate(sums))

    sums = lax.fori_loop(0, N_CTX, add_source, tuple(jnp.zeros((8, HD), F32) for _ in range(N_ADP)))
    for t in range(N_ADP):
        tbuf[t] = sums[t]

    def g_copy(i):
        to = rem(a + i, N_ADP)
        return pltpu.make_async_remote_copy(
            src_ref=tbuf.at[to], dst_ref=gbuf.at[a], send_sem=g_send, recv_sem=g_recv,
            device_id={"ctx": c, "adp": to}, device_id_type=MESH,
        )

    def g_all(sem):
        ref = gbuf.at[pl.ds(0, N_ADP - 1)]
        return pltpu.make_async_copy(ref, ref, sem)

    @pl.loop(1, N_ADP)
    def _(i):
        g_copy(i).start()

    gbuf[a] = tbuf[a]

    r_all(r_recv).wait()
    share = rbuf[0]
    for i in range(1, N_ADP):
        share = share + rbuf[i]
    glr_ref[...] = share[:, :RANK]
    out_glr = pltpu.make_async_copy(glr_ref, glr_hbm, out_sem.at[1])
    out_glr.start()
    wait_all(qbuf, p_send)
    r_all(r_send).wait()
    out_gq.wait()

    g_all(g_recv).wait()
    for i in range(N_ADP):
        tile = gbuf[i]
        ga_ref[0, pl.ds(i * 4, 4), :] = tile[0:4] + tile[4:8]
    out_ga = pltpu.make_async_copy(ga_ref, ga_hbm, out_sem.at[2])
    out_ga.start()
    g_all(g_send).wait()
    out_glr.wait()
    out_ga.wait()


def finish(gq_in, glr_in, ga_in, gq_out, glr_out, ga_out):
    gq_out[...] = gq_in[...]
    glr_out[...] = glr_in[...]
    ga_out[...] = ga_in[...]


def on_device(queries, keys, values, grad_out, docs, block_tenant, low_rank, adapter_b):
    anywhere = pl.BlockSpec(memory_space=pl.ANY)
    vmem = pl.BlockSpec(memory_space=pltpu.VMEM)
    dma = pltpu.SemaphoreType.DMA
    shapes = (
        jax.ShapeDtypeStruct((TOK, 2 * HD), BF16),
        jax.ShapeDtypeStruct((16, RANK), F32),
        jax.ShapeDtypeStruct((1, RANK, HD), F32),
    )
    grads = pl.pallas_call(
        body,
        out_shape=shapes,
        in_specs=[anywhere] * 8,
        out_specs=(anywhere,) * 3,
        scratch_shapes=[
            pltpu.VMEM((N_CTX, 2, SLOT, HD), BF16),
            pltpu.VMEM((SLOT, HD), BF16),
            pltpu.VMEM((TOK, 2 * HD), BF16),
            pltpu.VMEM((TOK, 2 * HD), BF16),
            pltpu.VMEM((2, HD), jnp.int32),
            pltpu.SMEM((2,), jnp.int32),
            pltpu.VMEM((RANK, TOK), BF16),
            pltpu.VMEM((TOK, 2 * HD), BF16),
            pltpu.VMEM((16, RANK), F32),
            pltpu.VMEM((1, RANK, HD), F32),
            pltpu.VMEM((2, 2 * TOK, 2 * HD), F32),
            pltpu.VMEM((2, TOK, HD), F32),
            pltpu.VMEM((TOK, HD), F32),
            pltpu.VMEM((N_ADP, RANK, 2 * HD), BF16),
            pltpu.VMEM((2, HD), jnp.int32),
            pltpu.VMEM((N_CTX, 2, HD), jnp.int32),
            pltpu.VMEM((2 * RANK, TOK), BF16),
            pltpu.VMEM((2, N_ADP, 8, HD), F32),
            pltpu.VMEM((N_CTX, 8, HD), F32),
            pltpu.VMEM((N_ADP, 8, HD), F32),
            pltpu.VMEM((N_ADP, 8, HD), F32),
            pltpu.VMEM((N_ADP, 16, HD), F32),
            pltpu.VMEM((N_ADP, 16, HD), F32),
            dma((9,)), dma((N_CTX,)), dma((N_CTX,)), dma((N_CTX,)), dma((N_CTX,)),
            dma((N_CTX,)), dma((N_CTX,)), dma((N_CTX,)), dma((3,)), dma((2,)),
            dma, dma, dma, dma, dma, dma, dma, dma, dma, dma, dma, dma, dma((3,)),
        ],
        compiler_params=pltpu.CompilerParams(
            collective_id=0, has_side_effects=True, vmem_limit_bytes=60 * 1024 * 1024
        ),
        cost_estimate=pl.CostEstimate(flops=4_000_000_000, bytes_accessed=4_000_000, transcendentals=4_000_000),
    )(
        queries, keys, values, grad_out, docs.reshape(2, HD), block_tenant, low_rank.T, adapter_b
    )
    return pl.pallas_call(
        finish,
        out_shape=shapes,
        in_specs=[vmem] * 3,
        out_specs=(vmem,) * 3,
        compiler_params=pltpu.CompilerParams(vmem_limit_bytes=60 * 1024 * 1024),
    )(*grads)


def solution(mesh):
    placed = (
        P("ctx", "adp"),
        P("ctx", None),
        P("ctx", None),
        P("ctx", "adp"),
        P("ctx"),
        P("ctx"),
        P("ctx", None),
        P("adp", None, None),
    )
    return jax.shard_map(
        on_device,
        mesh=mesh,
        in_specs=placed,
        out_specs=(P("ctx", "adp"), P(("ctx", "adp"), None), P("adp", None, "ctx")),
        check_vma=False,
    )
```

```python
import math

import jax
import jax.numpy as jnp
from jax import lax
from jax.experimental import pallas as pl
from jax.experimental.pallas import tpu as pltpu
from jax.sharding import PartitionSpec as P

HD = 128
RANK = 64
TOK = 256
NZ = 8
NX = 4
NYL = 4
N_CTX = 32
N_ADP = 16
SLOT = TOK + 16
HALF = TOK // 2
EXP2_SCALE = HD ** (-0.5) * math.log2(math.e)
FAR = -1e30
MESH = pl.DeviceIdType.MESH
ARRIVALS = (1, 7, 2, 6, 8 + 0, 8 + 2, 8 + 6, 3, 5, 8 + 1, 8 + 7, 8 + 3, 8 + 5, 4, 8 + 4)
ON_PLUS = sum(1 << code for code in (2, 8, 10, 11))
ON_MINUS = sum(1 << code for code in (6, 5, 8, 14))
Y_STEPS = (0, 2, -2,)
EARLY = sum(code << (4 * i) for i, code in enumerate(ARRIVALS[:7]))
LATE = sum(code << (4 * i) for i, code in enumerate(ARRIVALS[7:14]))
LAST = ARRIVALS[14]
LAG_SWAP, LAG_USE = 3, 5
F32 = jnp.float32
BF16 = jnp.bfloat16


def rem(value, by):
    return lax.rem(value, jnp.int32(by))


def div(value, by):
    return lax.div(value, jnp.int32(by))


def nt_dot(a, b):
    return lax.dot_general(a, b, (((1,), (1,)), ((), ())), preferred_element_type=F32)


def body(
    q_hbm, k_hbm, v_hbm, go_hbm, docs_hbm, bt_hbm, low_hbm, b_hbm,
    gq_hbm, glr_hbm, ga_hbm,
    kv, xkv, q_ref, go_ref, docs_ref, bt_ref, low_ref, gq_ref, glr_ref, ga_ref,
    acc, row_top, qdoc, bcols, bt_mine, btile, lowt, pbuf, qbuf, tbuf, gbuf, rsend, rbuf,
    loc_sem, mine_recv, other_recv, plus_send, minus_send, sib_send, sib2_send, x_send, y_send, far_send,
    bt_recv, bt_send, b_recv, b_send, bs_recv, bs_send,
    r_recv, r_send, p_recv, p_send, g_recv, g_send, out_sem,
):
    c = lax.axis_index("ctx")
    a = lax.axis_index("adp")
    core = rem(c, 2)
    pair = div(c, 2)
    z = rem(pair, NZ)
    y_hi = div(pair, NZ)
    head = div(a, NX)
    x = rem(a, NX)
    mine = rem(x, 2)
    other = 1 - mine
    sib = pair * 2 + (1 - core)
    z_plus = (y_hi * NZ + rem(z + 1, NZ)) * 2 + core
    z_minus = (y_hi * NZ + rem(z + NZ - 1, NZ)) * 2 + core
    z_far_plus = (y_hi * NZ + rem(z + 2, NZ)) * 2 + core
    z_far_minus = (y_hi * NZ + rem(z + NZ - 2, NZ)) * 2 + core
    x_plus = head * NX + rem(x + 1, NX)
    x_minus = head * NX + rem(x + NX - 1, NX)

    def y_ctx(step):
        return ((1 - y_hi) * NZ + rem(z + NZ + step, NZ)) * 2 + core

    y_adp = (NYL - 1 - head) * NX + x
    selfdest = (pair == a).astype(jnp.int32)

    barrier = pltpu.get_barrier_semaphore()

    def greet(ctx, adp):
        pl.semaphore_signal(barrier, inc=1, device_id={"ctx": ctx, "adp": adp}, device_id_type=MESH)

    greet(z_plus, a)
    greet(z_minus, a)
    greet(z_far_plus, a)
    greet(z_far_minus, a)
    greet(sib, a)

    @pl.when(y_hi == 1)
    def _():
        for step in Y_STEPS:
            greet(y_ctx(step), y_adp)

    @pl.loop(1, N_ADP)
    def _(i):
        greet(c, rem(a + i, N_ADP))

    @pl.loop(0, N_CTX)
    def _(i):
        @pl.when(jnp.logical_not((pair == a) & (i == c)))
        def _():
            greet(i, pair)

    def col(which):
        return pl.ds(pl.multiple_of(which * HD, HD), HD)

    far_head = NYL - 1 - head
    get_docs = pltpu.make_async_copy(docs_hbm, docs_ref, loc_sem.at[0])
    own_k = pltpu.make_async_copy(k_hbm.at[:, col(head)], kv.at[c, 0, pl.ds(0, TOK)], loc_sem.at[1])
    own_v = pltpu.make_async_copy(v_hbm.at[:, col(head)], kv.at[c, 1, pl.ds(0, TOK)], loc_sem.at[2])
    x_k = pltpu.make_async_copy(k_hbm.at[:, col(far_head)], xkv.at[pl.ds(0, TOK)], loc_sem.at[3])
    x_v = pltpu.make_async_copy(v_hbm.at[:, col(far_head)], xkv.at[pl.ds(0, TOK)], loc_sem.at[3])
    get_q = pltpu.make_async_copy(q_hbm, q_ref, loc_sem.at[4])
    get_go = pltpu.make_async_copy(go_hbm, go_ref, loc_sem.at[5])
    get_bt = pltpu.make_async_copy(bt_hbm, bt_ref, loc_sem.at[6])
    get_low = pltpu.make_async_copy(low_hbm, low_ref, loc_sem.at[7])
    half = pl.multiple_of(core * (RANK // 2), RANK // 2)
    own_b = pltpu.make_async_copy(
        b_hbm.at[0, pl.ds(half, RANK // 2), pl.ds(pl.multiple_of(a * 2 * HD, 2 * HD), 2 * HD)],
        bcols.at[a, pl.ds(half, RANK // 2)],
        loc_sem.at[8],
    )
    get_docs.start()
    own_k.start()
    own_v.start()

    @pl.when(mine == 0)
    def _():
        x_k.start()

    @pl.when(mine == 1)
    def _():
        x_v.start()

    get_bt.start()
    get_q.start()
    get_go.start()
    get_low.start()
    own_b.start()

    get_docs.wait()
    doc_rows = docs_ref[...].astype(F32)
    tag = jnp.concatenate([doc_rows, jnp.zeros((14, HD), F32)], axis=0).astype(BF16)
    kv[c, mine, pl.ds(TOK, 16), :] = tag
    xkv[pl.ds(TOK, 16), :] = tag
    own_k.wait()
    own_v.wait()
    x_k.wait()
    pl.semaphore_wait(barrier, 5 + len(Y_STEPS) * (1 - y_hi) + (N_ADP - 1) + N_CTX - selfdest)

    def along(chunk, send_sem, to):
        ref = kv.at[chunk, mine]
        return pltpu.make_async_remote_copy(
            src_ref=ref, dst_ref=ref, send_sem=send_sem.at[chunk], recv_sem=mine_recv.at[chunk],
            device_id={"ctx": to, "adp": a}, device_id_type=MESH,
        )

    def rest_to_sib(chunk):
        ref = kv.at[chunk, other, pl.ds(0, TOK)]
        return pltpu.make_async_remote_copy(
            src_ref=ref, dst_ref=ref, send_sem=sib2_send.at[chunk], recv_sem=other_recv.at[chunk],
            device_id={"ctx": sib, "adp": a}, device_id_type=MESH,
        )

    def swap(chunk, first, to):
        ref = kv.at[chunk, mine, pl.ds(first, HALF)]
        return pltpu.make_async_remote_copy(
            src_ref=ref, dst_ref=ref, send_sem=x_send.at[chunk], recv_sem=other_recv.at[chunk],
            device_id={"ctx": c, "adp": to}, device_id_type=MESH,
        )

    def to_y(which):
        return pltpu.make_async_remote_copy(
            src_ref=xkv, dst_ref=kv.at[c, mine], send_sem=y_send.at[which], recv_sem=mine_recv.at[c],
            device_id={"ctx": y_ctx(Y_STEPS[which]), "adp": y_adp}, device_id_type=MESH,
        )

    def far(which):
        ref = kv.at[c, mine]
        return pltpu.make_async_remote_copy(
            src_ref=ref, dst_ref=ref, send_sem=far_send.at[which], recv_sem=mine_recv.at[c],
            device_id={"ctx": (z_far_plus, z_far_minus)[which], "adp": a}, device_id_type=MESH,
        )

    def await_mine(chunk):
        ref = kv.at[chunk, mine]
        pltpu.make_async_copy(ref, ref, mine_recv.at[chunk]).wait()

    def await_other(chunk):
        ref = kv.at[chunk, other, pl.ds(0, TOK)]
        pltpu.make_async_copy(ref, ref, other_recv.at[chunk]).wait()

    def await_swap_sent(chunk):
        ref = kv.at[chunk, mine, pl.ds(0, TOK)]
        pltpu.make_async_copy(ref, ref, x_send.at[chunk]).wait()

    along(c, plus_send, z_plus).start()
    along(c, minus_send, z_minus).start()

    far(0).start()
    far(1).start()

    @pl.when(y_hi == 0)
    def _():
        for which in range(len(Y_STEPS)):
            to_y(which).start()

    along(c, sib_send, sib).start()
    rest_to_sib(c).start()

    def b_copy(i):
        to = rem(a + i, N_ADP)
        return pltpu.make_async_remote_copy(
            src_ref=b_hbm.at[0, pl.ds(half, RANK // 2), pl.ds(pl.multiple_of(to * 2 * HD, 2 * HD), 2 * HD)],
            dst_ref=bcols.at[a, pl.ds(half, RANK // 2)],
            send_sem=b_send, recv_sem=b_recv,
            device_id={"ctx": c, "adp": to}, device_id_type=MESH,
        )

    def b_all(sem):
        ref = bcols.at[pl.ds(0, N_ADP - 1), pl.ds(half, RANK // 2)]
        return pltpu.make_async_copy(ref, ref, sem)

    def b_share():
        ref = bcols.at[:, pl.ds(half, RANK // 2)]
        return pltpu.make_async_remote_copy(
            src_ref=ref, dst_ref=ref, send_sem=bs_send, recv_sem=bs_recv,
            device_id={"ctx": sib, "adp": a}, device_id_type=MESH,
        )

    def b_shared():
        ref = bcols.at[:, pl.ds(pl.multiple_of((1 - core) * (RANK // 2), RANK // 2), RANK // 2)]
        return pltpu.make_async_copy(ref, ref, bs_recv)

    @pl.loop(1, N_ADP)
    def _(i):
        b_copy(i).start()

    get_bt.wait()
    bt_mine[...] = jnp.where(lax.broadcasted_iota(jnp.int32, (2, HD), 0) == 0, bt_ref[0], bt_ref[1])

    def to_sum(i):
        return a * 2 + rem(i, 2), rem(a + div(i, 2), N_ADP)

    def bt_copy(i):
        ctx, adp = to_sum(i)
        return pltpu.make_async_remote_copy(
            src_ref=bt_mine, dst_ref=btile.at[c], send_sem=bt_send, recv_sem=bt_recv,
            device_id={"ctx": ctx, "adp": adp}, device_id_type=MESH,
        )

    def wait_all(buffer, sem):
        @pl.when(selfdest == 0)
        def _():
            pltpu.make_async_copy(buffer, buffer, sem).wait()

        @pl.when(selfdest == 1)
        def _():
            ref = buffer.at[pl.ds(0, N_CTX - 1)]
            pltpu.make_async_copy(ref, ref, sem).wait()

    def is_self(i):
        return (selfdest == 1) & (i == core)

    @pl.loop(0, N_CTX)
    def _(i):
        @pl.when(jnp.logical_not(is_self(i)))
        def _():
            bt_copy(i).start()

    @pl.when(selfdest == 1)
    def _():
        btile[c] = bt_mine[...]

    get_low.wait()
    rr = lax.broadcasted_iota(jnp.int32, (2 * RANK, RANK), 0)
    kk = lax.broadcasted_iota(jnp.int32, (2 * RANK, RANK), 1)
    pick = jnp.where(kk == ((rr >> 3) * 4 + (rr & 3)), 1.0, 0.0).astype(BF16)
    spread = jnp.dot(pick, low_ref[...], preferred_element_type=F32)
    rr = lax.broadcasted_iota(jnp.int32, (2 * RANK, TOK), 0)
    tt = lax.broadcasted_iota(jnp.int32, (2 * RANK, TOK), 1)
    lowt[...] = jnp.where((tt >> 7) == ((rr >> 2) & 1), spread, 0.0).astype(BF16)

    ri = lax.broadcasted_iota(jnp.int32, (HD, HD), 0)
    ci = lax.broadcasted_iota(jnp.int32, (HD, HD), 1)
    for part in range(2):
        spot = jnp.where(ri == ci, jnp.broadcast_to(doc_rows[part : part + 1, :], (HD, HD)), 0.0)
        column = jnp.sum(spot, axis=1, keepdims=True)
        qdoc[pl.ds(part * HD, HD), :] = jnp.broadcast_to(column, (HD, HD))

    ones = jnp.ones((TOK, HD), BF16)

    def attend(which, first):
        low_slot = which * 2
        row_doc = qdoc[...]
        for h in range(2):
            q_h = q_ref[:, h * HD : (h + 1) * HD]
            g_h = go_ref[:, h * HD : (h + 1) * HD]
            tiles = []
            for half_pair in range(2):
                scores = nt_dot(q_h, kv[low_slot + half_pair, 0, pl.ds(0, TOK), :])
                key_doc = kv[low_slot + half_pair, mine, pl.ds(TOK, 16), :].astype(F32)
                for lt in range(2):
                    seen = row_doc == key_doc[lt : lt + 1, :]
                    if first:
                        rpos = lax.broadcasted_iota(jnp.int32, (TOK, HD), 0) + core * TOK
                        kpos = lax.broadcasted_iota(jnp.int32, (TOK, HD), 1) + (half_pair * TOK + lt * HD)
                        seen = seen & (kpos <= rpos)
                    tiles.append(jnp.where(seen, scores[:, lt * HD : (lt + 1) * HD], FAR))
            top = jnp.maximum(jnp.maximum(tiles[0], tiles[1]), jnp.maximum(tiles[2], tiles[3]))
            top = jnp.broadcast_to(jnp.max(top, axis=1, keepdims=True), (TOK, HD))
            if not first:
                before = row_top[h]
                top = jnp.maximum(top, before)
                decay = jnp.exp2((before - top) * EXP2_SCALE)
            row_top[h] = top
            total = None
            for half_pair in range(2):
                weights = [
                    jnp.exp2((tiles[half_pair * 2 + lt] - top) * EXP2_SCALE) for lt in range(2)
                ]
                weights = jnp.concatenate(weights, axis=1)
                gw = nt_dot(g_h, kv[low_slot + half_pair, 1, pl.ds(0, TOK), :])
                both = jnp.concatenate([weights.astype(BF16), (weights * gw).astype(BF16)], axis=0)
                right = jnp.concatenate([kv[low_slot + half_pair, 0, pl.ds(0, TOK), :], ones], axis=1)
                term = jnp.dot(both, right, preferred_element_type=F32)
                total = term if total is None else total + term
            if first:
                acc[h] = total
            else:
                wide = jnp.concatenate([decay, decay], axis=1)
                wide = jnp.concatenate([wide, wide], axis=0)
                acc[h] = acc[h] * wide + total

    get_q.wait()
    get_go.wait()
    await_mine(sib)
    await_other(sib)
    attend(pair, True)

    def event(e):
        e_low = jnp.clip(e, 0, 6)
        e_high = jnp.clip(e - 7, 0, 6)
        code = jnp.where(
            e < 7, lax.shift_right_logical(jnp.int32(EARLY), 4 * e_low),
            jnp.where(e < 14, lax.shift_right_logical(jnp.int32(LATE), 4 * e_high), LAST),
        )
        code = code & 15
        lower, off = div(code, 8), rem(code, 8)
        valid = (e >= 0) & (e < len(ARRIVALS)) & (lower <= y_hi)
        src_pair = (y_hi - lower) * NZ + rem(z + NZ - off, NZ)
        on_plus = valid & ((lax.shift_right_logical(jnp.int32(ON_PLUS), code) & 1) == 1)
        on_minus = valid & ((lax.shift_right_logical(jnp.int32(ON_MINUS), code) & 1) == 1)
        return valid, src_pair, on_plus, on_minus

    @pl.loop(0, len(ARRIVALS) + LAG_USE)
    def _(e):
        valid, src_pair, on_plus, on_minus = event(e)
        chunk = src_pair * 2 + core

        @pl.when(valid)
        def _():
            await_mine(chunk)

            @pl.when(on_plus)
            def _():
                along(chunk, plus_send, z_plus).start()

            @pl.when(on_minus)
            def _():
                along(chunk, minus_send, z_minus).start()

            swap(chunk, 0, x_plus).start()
            swap(chunk, HALF, x_minus).start()
            along(chunk, sib_send, sib).start()

        ready, src_pair, _, _ = event(e - LAG_SWAP)
        chunk2 = src_pair * 2 + core

        @pl.when(ready)
        def _():
            await_other(chunk2)
            rest_to_sib(chunk2).start()

        whole, last_pair, _, _ = event(e - LAG_USE)

        @pl.when(whole)
        def _():
            await_mine(last_pair * 2 + 1 - core)
            await_other(last_pair * 2 + 1 - core)

        @pl.when(whole & (last_pair < pair))
        def _():
            attend(last_pair, False)

    b_all(b_recv).wait()
    own_b.wait()
    b_share().start()

    for h in range(2):
        total = acc[h, pl.ds(0, TOK), pl.ds(HD, HD)]
        inv = 1.0 / total
        delta = acc[h, pl.ds(TOK, TOK), pl.ds(HD, HD)] * inv
        grad = (acc[h, pl.ds(TOK, TOK), pl.ds(0, HD)] - delta * acc[h, pl.ds(0, TOK), pl.ds(0, HD)]) * inv
        gq_ref[:, h * HD : (h + 1) * HD] = (grad * HD ** (-0.5)).astype(BF16)

    gq = gq_ref[...]
    partial = jnp.dot(lowt[...], gq, preferred_element_type=F32) * 2.0
    for h in range(2):
        pbuf[h] = partial[:, h * HD : (h + 1) * HD].reshape(N_ADP, 8, HD)

    def p_copy(i):
        ctx, adp = to_sum(i)
        return pltpu.make_async_remote_copy(
            src_ref=pbuf.at[rem(i, 2), adp], dst_ref=qbuf.at[c],
            send_sem=p_send, recv_sem=p_recv,
            device_id={"ctx": ctx, "adp": adp}, device_id_type=MESH,
        )

    @pl.loop(0, N_CTX)
    def _(i):
        @pl.when(jnp.logical_not(is_self(i)))
        def _():
            p_copy(i).start()

    @pl.when(selfdest == 1)
    def _():
        qbuf[c] = pbuf[core, a]

    out_gq = pltpu.make_async_copy(gq_ref, gq_hbm, out_sem.at[0])
    out_gq.start()

    b_shared().wait()
    for blk in range(2):
        chosen = bcols[bt_ref[blk]]
        padded = jnp.concatenate([chosen, jnp.zeros_like(chosen)], axis=0)
        part = nt_dot(gq[blk * HD : (blk + 1) * HD, :], padded) * 2.0
        rsend[pl.ds(blk * 8, 8)] = part.reshape(8, 16, HD)

    def r_copy(i):
        to = rem(a + i, N_ADP)
        return pltpu.make_async_remote_copy(
            src_ref=rsend.at[to], dst_ref=rbuf.at[a], send_sem=r_send, recv_sem=r_recv,
            device_id={"ctx": c, "adp": to}, device_id_type=MESH,
        )

    def r_all(sem):
        ref = rbuf.at[pl.ds(0, N_ADP - 1)]
        return pltpu.make_async_copy(ref, ref, sem)

    @pl.loop(1, N_ADP)
    def _(i):
        r_copy(i).start()

    rbuf[a] = rsend[a]

    wait_all(btile, bt_recv)
    wait_all(btile, bt_send)
    b_all(b_send).wait()
    b_share().wait_send()
    along(c, plus_send, z_plus).wait_send()
    along(c, minus_send, z_minus).wait_send()
    along(c, sib_send, sib).wait_send()
    rest_to_sib(c).wait_send()

    far(0).wait_send()
    far(1).wait_send()

    @pl.when(y_hi == 0)
    def _():
        for which in range(len(Y_STEPS)):
            to_y(which).wait_send()

    @pl.loop(0, len(ARRIVALS))
    def _(e):
        valid, src_pair, on_plus, on_minus = event(e)
        chunk = src_pair * 2 + core

        @pl.when(on_plus)
        def _():
            along(chunk, plus_send, z_plus).wait_send()

        @pl.when(on_minus)
        def _():
            along(chunk, minus_send, z_minus).wait_send()

        @pl.when(valid)
        def _():
            await_swap_sent(chunk)
            along(chunk, sib_send, sib).wait_send()
            rest_to_sib(chunk).wait_send()

    wait_all(qbuf, p_recv)
    upper = lax.broadcasted_iota(jnp.int32, (8, HD), 0) < 4

    def add_source(i, sums):
        tile = qbuf[i]
        owner = jnp.where(
            upper, jnp.broadcast_to(btile[i, 0:1, :], (8, HD)), jnp.broadcast_to(btile[i, 1:2, :], (8, HD))
        )
        return tuple(s + jnp.where(owner == t, tile, 0.0) for t, s in enumerate(sums))

    sums = lax.fori_loop(0, N_CTX, add_source, tuple(jnp.zeros((8, HD), F32) for _ in range(N_ADP)))
    for t in range(N_ADP):
        tbuf[t] = sums[t]

    def g_copy(i):
        to = rem(a + i, N_ADP)
        return pltpu.make_async_remote_copy(
            src_ref=tbuf.at[to], dst_ref=gbuf.at[a], send_sem=g_send, recv_sem=g_recv,
            device_id={"ctx": c, "adp": to}, device_id_type=MESH,
        )

    def g_all(sem):
        ref = gbuf.at[pl.ds(0, N_ADP - 1)]
        return pltpu.make_async_copy(ref, ref, sem)

    @pl.loop(1, N_ADP)
    def _(i):
        g_copy(i).start()

    gbuf[a] = tbuf[a]

    r_all(r_recv).wait()
    share = rbuf[0]
    for i in range(1, N_ADP):
        share = share + rbuf[i]
    glr_ref[...] = share[:, :RANK]
    out_glr = pltpu.make_async_copy(glr_ref, glr_hbm, out_sem.at[1])
    out_glr.start()
    wait_all(qbuf, p_send)
    r_all(r_send).wait()
    out_gq.wait()

    g_all(g_recv).wait()
    for i in range(N_ADP):
        tile = gbuf[i]
        ga_ref[0, pl.ds(i * 4, 4), :] = tile[0:4] + tile[4:8]
    out_ga = pltpu.make_async_copy(ga_ref, ga_hbm, out_sem.at[2])
    out_ga.start()
    g_all(g_send).wait()
    out_glr.wait()
    out_ga.wait()


def finish(gq_in, glr_in, ga_in, gq_out, glr_out, ga_out):
    gq_out[...] = gq_in[...]
    glr_out[...] = glr_in[...]
    ga_out[...] = ga_in[...]


def on_device(queries, keys, values, grad_out, docs, block_tenant, low_rank, adapter_b):
    anywhere = pl.BlockSpec(memory_space=pl.ANY)
    vmem = pl.BlockSpec(memory_space=pltpu.VMEM)
    dma = pltpu.SemaphoreType.DMA
    shapes = (
        jax.ShapeDtypeStruct((TOK, 2 * HD), BF16),
        jax.ShapeDtypeStruct((16, RANK), F32),
        jax.ShapeDtypeStruct((1, RANK, HD), F32),
    )
    grads = pl.pallas_call(
        body,
        out_shape=shapes,
        in_specs=[anywhere] * 8,
        out_specs=(anywhere,) * 3,
        scratch_shapes=[
            pltpu.VMEM((N_CTX, 2, SLOT, HD), BF16),
            pltpu.VMEM((SLOT, HD), BF16),
            pltpu.VMEM((TOK, 2 * HD), BF16),
            pltpu.VMEM((TOK, 2 * HD), BF16),
            pltpu.VMEM((2, HD), jnp.int32),
            pltpu.SMEM((2,), jnp.int32),
            pltpu.VMEM((RANK, TOK), BF16),
            pltpu.VMEM((TOK, 2 * HD), BF16),
            pltpu.VMEM((16, RANK), F32),
            pltpu.VMEM((1, RANK, HD), F32),
            pltpu.VMEM((2, 2 * TOK, 2 * HD), F32),
            pltpu.VMEM((2, TOK, HD), F32),
            pltpu.VMEM((TOK, HD), F32),
            pltpu.VMEM((N_ADP, RANK, 2 * HD), BF16),
            pltpu.VMEM((2, HD), jnp.int32),
            pltpu.VMEM((N_CTX, 2, HD), jnp.int32),
            pltpu.VMEM((2 * RANK, TOK), BF16),
            pltpu.VMEM((2, N_ADP, 8, HD), F32),
            pltpu.VMEM((N_CTX, 8, HD), F32),
            pltpu.VMEM((N_ADP, 8, HD), F32),
            pltpu.VMEM((N_ADP, 8, HD), F32),
            pltpu.VMEM((N_ADP, 16, HD), F32),
            pltpu.VMEM((N_ADP, 16, HD), F32),
            dma((9,)), dma((N_CTX,)), dma((N_CTX,)), dma((N_CTX,)), dma((N_CTX,)),
            dma((N_CTX,)), dma((N_CTX,)), dma((N_CTX,)), dma((len(Y_STEPS),)), dma((2,)),
            dma, dma, dma, dma, dma, dma, dma, dma, dma, dma, dma, dma, dma((3,)),
        ],
        compiler_params=pltpu.CompilerParams(
            collective_id=0, has_side_effects=True, vmem_limit_bytes=60 * 1024 * 1024
        ),
        cost_estimate=pl.CostEstimate(flops=4_000_000_000, bytes_accessed=4_000_000, transcendentals=4_000_000),
    )(
        queries, keys, values, grad_out, docs.reshape(2, HD), block_tenant, low_rank.T, adapter_b
    )
    return pl.pallas_call(
        finish,
        out_shape=shapes,
        in_specs=[vmem] * 3,
        out_specs=(vmem,) * 3,
        compiler_params=pltpu.CompilerParams(vmem_limit_bytes=60 * 1024 * 1024),
    )(*grads)


def solution(mesh):
    placed = (
        P("ctx", "adp"),
        P("ctx", None),
        P("ctx", None),
        P("ctx", "adp"),
        P("ctx"),
        P("ctx"),
        P("ctx", None),
        P("adp", None, None),
    )
    return jax.shard_map(
        on_device,
        mesh=mesh,
        in_specs=placed,
        out_specs=(P("ctx", "adp"), P(("ctx", "adp"), None), P("adp", None, "ctx")),
        check_vma=False,
    )
```

```python
import math

import jax
import jax.numpy as jnp
from jax import lax
from jax.experimental import pallas as pl
from jax.experimental.pallas import tpu as pltpu
from jax.sharding import PartitionSpec as P

HD = 128
RANK = 64
TOK = 256
NZ = 8
NX = 4
NYL = 4
N_CTX = 32
N_ADP = 16
SLOT = TOK + 16
HALF = TOK // 2
EXP2_SCALE = HD ** (-0.5) * math.log2(math.e)
FAR = -1e30
MESH = pl.DeviceIdType.MESH
ARRIVALS = (1, 7, 2, 6, 8 + 0, 8 + 2, 8 + 6, 3, 5, 8 + 1, 8 + 7, 8 + 3, 8 + 5, 4, 8 + 4)
ON_PLUS = sum(1 << code for code in (2, 8, 10, 11))
ON_MINUS = sum(1 << code for code in (6, 5, 8, 14))
Y_STEPS = (0, 2, -2,)
EARLY = sum(code << (4 * i) for i, code in enumerate(ARRIVALS[:7]))
LATE = sum(code << (4 * i) for i, code in enumerate(ARRIVALS[7:14]))
LAST = ARRIVALS[14]
LAG_SWAP, LAG_USE = 2, 4
F32 = jnp.float32
BF16 = jnp.bfloat16


def rem(value, by):
    return lax.rem(value, jnp.int32(by))


def div(value, by):
    return lax.div(value, jnp.int32(by))


def nt_dot(a, b):
    return lax.dot_general(a, b, (((1,), (1,)), ((), ())), preferred_element_type=F32)


def body(
    q_hbm, k_hbm, v_hbm, go_hbm, docs_hbm, bt_hbm, low_hbm, b_hbm,
    gq_hbm, glr_hbm, ga_hbm,
    kv, xkv, q_ref, go_ref, docs_ref, bt_ref, low_ref, gq_ref, glr_ref, ga_ref,
    acc, row_top, qdoc, bcols, bt_mine, btile, lowt, pbuf, qbuf, tbuf, gbuf, rsend, rbuf,
    loc_sem, mine_recv, other_recv, plus_send, minus_send, sib_send, sib2_send, x_send, y_send, far_send,
    bt_recv, bt_send, b_recv, b_send, bs_recv, bs_send,
    r_recv, r_send, p_recv, p_send, g_recv, g_send, out_sem,
):
    c = lax.axis_index("ctx")
    a = lax.axis_index("adp")
    core = rem(c, 2)
    pair = div(c, 2)
    z = rem(pair, NZ)
    y_hi = div(pair, NZ)
    head = div(a, NX)
    x = rem(a, NX)
    mine = rem(x, 2)
    other = 1 - mine
    sib = pair * 2 + (1 - core)
    z_plus = (y_hi * NZ + rem(z + 1, NZ)) * 2 + core
    z_minus = (y_hi * NZ + rem(z + NZ - 1, NZ)) * 2 + core
    z_far_plus = (y_hi * NZ + rem(z + 2, NZ)) * 2 + core
    z_far_minus = (y_hi * NZ + rem(z + NZ - 2, NZ)) * 2 + core
    x_plus = head * NX + rem(x + 1, NX)
    x_minus = head * NX + rem(x + NX - 1, NX)

    def y_ctx(step):
        return ((1 - y_hi) * NZ + rem(z + NZ + step, NZ)) * 2 + core

    y_adp = (NYL - 1 - head) * NX + x
    selfdest = (pair == a).astype(jnp.int32)

    barrier = pltpu.get_barrier_semaphore()

    def greet(ctx, adp):
        pl.semaphore_signal(barrier, inc=1, device_id={"ctx": ctx, "adp": adp}, device_id_type=MESH)

    greet(z_plus, a)
    greet(z_minus, a)
    greet(z_far_plus, a)
    greet(z_far_minus, a)
    greet(sib, a)

    @pl.when(y_hi == 1)
    def _():
        for step in Y_STEPS:
            greet(y_ctx(step), y_adp)

    @pl.loop(1, N_ADP)
    def _(i):
        greet(c, rem(a + i, N_ADP))

    @pl.loop(0, N_CTX)
    def _(i):
        @pl.when(jnp.logical_not((pair == a) & (i == c)))
        def _():
            greet(i, pair)

    def col(which):
        return pl.ds(pl.multiple_of(which * HD, HD), HD)

    far_head = NYL - 1 - head
    get_docs = pltpu.make_async_copy(docs_hbm, docs_ref, loc_sem.at[0])
    own_k = pltpu.make_async_copy(k_hbm.at[:, col(head)], kv.at[c, 0, pl.ds(0, TOK)], loc_sem.at[1])
    own_v = pltpu.make_async_copy(v_hbm.at[:, col(head)], kv.at[c, 1, pl.ds(0, TOK)], loc_sem.at[2])
    x_k = pltpu.make_async_copy(k_hbm.at[:, col(far_head)], xkv.at[pl.ds(0, TOK)], loc_sem.at[3])
    x_v = pltpu.make_async_copy(v_hbm.at[:, col(far_head)], xkv.at[pl.ds(0, TOK)], loc_sem.at[3])
    get_q = pltpu.make_async_copy(q_hbm, q_ref, loc_sem.at[4])
    get_go = pltpu.make_async_copy(go_hbm, go_ref, loc_sem.at[5])
    get_bt = pltpu.make_async_copy(bt_hbm, bt_ref, loc_sem.at[6])
    get_low = pltpu.make_async_copy(low_hbm, low_ref, loc_sem.at[7])
    half = pl.multiple_of(core * (RANK // 2), RANK // 2)
    own_b = pltpu.make_async_copy(
        b_hbm.at[0, pl.ds(half, RANK // 2), pl.ds(pl.multiple_of(a * 2 * HD, 2 * HD), 2 * HD)],
        bcols.at[a, pl.ds(half, RANK // 2)],
        loc_sem.at[8],
    )
    get_docs.start()
    own_k.start()
    own_v.start()

    @pl.when(mine == 0)
    def _():
        x_k.start()

    @pl.when(mine == 1)
    def _():
        x_v.start()

    get_bt.start()
    get_q.start()
    get_go.start()
    get_low.start()
    own_b.start()

    get_docs.wait()
    doc_rows = docs_ref[...].astype(F32)
    tag = jnp.concatenate([doc_rows, jnp.zeros((14, HD), F32)], axis=0).astype(BF16)
    kv[c, mine, pl.ds(TOK, 16), :] = tag
    xkv[pl.ds(TOK, 16), :] = tag
    own_k.wait()
    own_v.wait()
    x_k.wait()
    pl.semaphore_wait(barrier, 5 + len(Y_STEPS) * (1 - y_hi) + (N_ADP - 1) + N_CTX - selfdest)

    def along(chunk, send_sem, to):
        ref = kv.at[chunk, mine]
        return pltpu.make_async_remote_copy(
            src_ref=ref, dst_ref=ref, send_sem=send_sem.at[chunk], recv_sem=mine_recv.at[chunk],
            device_id={"ctx": to, "adp": a}, device_id_type=MESH,
        )

    def rest_to_sib(chunk):
        ref = kv.at[chunk, other, pl.ds(0, TOK)]
        return pltpu.make_async_remote_copy(
            src_ref=ref, dst_ref=ref, send_sem=sib2_send.at[chunk], recv_sem=other_recv.at[chunk],
            device_id={"ctx": sib, "adp": a}, device_id_type=MESH,
        )

    def swap(chunk, first, to):
        ref = kv.at[chunk, mine, pl.ds(first, HALF)]
        return pltpu.make_async_remote_copy(
            src_ref=ref, dst_ref=ref, send_sem=x_send.at[chunk], recv_sem=other_recv.at[chunk],
            device_id={"ctx": c, "adp": to}, device_id_type=MESH,
        )

    def to_y(which):
        return pltpu.make_async_remote_copy(
            src_ref=xkv, dst_ref=kv.at[c, mine], send_sem=y_send.at[which], recv_sem=mine_recv.at[c],
            device_id={"ctx": y_ctx(Y_STEPS[which]), "adp": y_adp}, device_id_type=MESH,
        )

    def far(which):
        ref = kv.at[c, mine]
        return pltpu.make_async_remote_copy(
            src_ref=ref, dst_ref=ref, send_sem=far_send.at[which], recv_sem=mine_recv.at[c],
            device_id={"ctx": (z_far_plus, z_far_minus)[which], "adp": a}, device_id_type=MESH,
        )

    def await_mine(chunk):
        ref = kv.at[chunk, mine]
        pltpu.make_async_copy(ref, ref, mine_recv.at[chunk]).wait()

    def await_other(chunk):
        ref = kv.at[chunk, other, pl.ds(0, TOK)]
        pltpu.make_async_copy(ref, ref, other_recv.at[chunk]).wait()

    def await_swap_sent(chunk):
        ref = kv.at[chunk, mine, pl.ds(0, TOK)]
        pltpu.make_async_copy(ref, ref, x_send.at[chunk]).wait()

    along(c, plus_send, z_plus).start()
    along(c, minus_send, z_minus).start()

    far(0).start()
    far(1).start()

    @pl.when(y_hi == 0)
    def _():
        for which in range(len(Y_STEPS)):
            to_y(which).start()

    along(c, sib_send, sib).start()
    rest_to_sib(c).start()

    def b_copy(i):
        to = rem(a + i, N_ADP)
        return pltpu.make_async_remote_copy(
            src_ref=b_hbm.at[0, pl.ds(half, RANK // 2), pl.ds(pl.multiple_of(to * 2 * HD, 2 * HD), 2 * HD)],
            dst_ref=bcols.at[a, pl.ds(half, RANK // 2)],
            send_sem=b_send, recv_sem=b_recv,
            device_id={"ctx": c, "adp": to}, device_id_type=MESH,
        )

    def b_all(sem):
        ref = bcols.at[pl.ds(0, N_ADP - 1), pl.ds(half, RANK // 2)]
        return pltpu.make_async_copy(ref, ref, sem)

    def b_share():
        ref = bcols.at[:, pl.ds(half, RANK // 2)]
        return pltpu.make_async_remote_copy(
            src_ref=ref, dst_ref=ref, send_sem=bs_send, recv_sem=bs_recv,
            device_id={"ctx": sib, "adp": a}, device_id_type=MESH,
        )

    def b_shared():
        ref = bcols.at[:, pl.ds(pl.multiple_of((1 - core) * (RANK // 2), RANK // 2), RANK // 2)]
        return pltpu.make_async_copy(ref, ref, bs_recv)

    @pl.loop(1, N_ADP)
    def _(i):
        b_copy(i).start()

    get_bt.wait()
    bt_mine[...] = jnp.where(lax.broadcasted_iota(jnp.int32, (2, HD), 0) == 0, bt_ref[0], bt_ref[1])

    def to_sum(i):
        return a * 2 + rem(i, 2), rem(a + div(i, 2), N_ADP)

    def bt_copy(i):
        ctx, adp = to_sum(i)
        return pltpu.make_async_remote_copy(
            src_ref=bt_mine, dst_ref=btile.at[c], send_sem=bt_send, recv_sem=bt_recv,
            device_id={"ctx": ctx, "adp": adp}, device_id_type=MESH,
        )

    def wait_all(buffer, sem):
        @pl.when(selfdest == 0)
        def _():
            pltpu.make_async_copy(buffer, buffer, sem).wait()

        @pl.when(selfdest == 1)
        def _():
            ref = buffer.at[pl.ds(0, N_CTX - 1)]
            pltpu.make_async_copy(ref, ref, sem).wait()

    def is_self(i):
        return (selfdest == 1) & (i == core)

    @pl.loop(0, N_CTX)
    def _(i):
        @pl.when(jnp.logical_not(is_self(i)))
        def _():
            bt_copy(i).start()

    @pl.when(selfdest == 1)
    def _():
        btile[c] = bt_mine[...]

    get_low.wait()
    rr = lax.broadcasted_iota(jnp.int32, (2 * RANK, RANK), 0)
    kk = lax.broadcasted_iota(jnp.int32, (2 * RANK, RANK), 1)
    pick = jnp.where(kk == ((rr >> 3) * 4 + (rr & 3)), 1.0, 0.0).astype(BF16)
    spread = jnp.dot(pick, low_ref[...], preferred_element_type=F32)
    rr = lax.broadcasted_iota(jnp.int32, (2 * RANK, TOK), 0)
    tt = lax.broadcasted_iota(jnp.int32, (2 * RANK, TOK), 1)
    lowt[...] = jnp.where((tt >> 7) == ((rr >> 2) & 1), spread, 0.0).astype(BF16)

    ri = lax.broadcasted_iota(jnp.int32, (HD, HD), 0)
    ci = lax.broadcasted_iota(jnp.int32, (HD, HD), 1)
    for part in range(2):
        spot = jnp.where(ri == ci, jnp.broadcast_to(doc_rows[part : part + 1, :], (HD, HD)), 0.0)
        column = jnp.sum(spot, axis=1, keepdims=True)
        qdoc[pl.ds(part * HD, HD), :] = jnp.broadcast_to(column, (HD, HD))

    ones = jnp.ones((TOK, HD), BF16)

    def attend(which, first):
        low_slot = which * 2
        row_doc = qdoc[...]
        for h in range(2):
            q_h = q_ref[:, h * HD : (h + 1) * HD]
            g_h = go_ref[:, h * HD : (h + 1) * HD]
            tiles = []
            for half_pair in range(2):
                scores = nt_dot(q_h, kv[low_slot + half_pair, 0, pl.ds(0, TOK), :])
                key_doc = kv[low_slot + half_pair, mine, pl.ds(TOK, 16), :].astype(F32)
                for lt in range(2):
                    seen = row_doc == key_doc[lt : lt + 1, :]
                    if first:
                        rpos = lax.broadcasted_iota(jnp.int32, (TOK, HD), 0) + core * TOK
                        kpos = lax.broadcasted_iota(jnp.int32, (TOK, HD), 1) + (half_pair * TOK + lt * HD)
                        seen = seen & (kpos <= rpos)
                    tiles.append(jnp.where(seen, scores[:, lt * HD : (lt + 1) * HD], FAR))
            top = jnp.maximum(jnp.maximum(tiles[0], tiles[1]), jnp.maximum(tiles[2], tiles[3]))
            top = jnp.broadcast_to(jnp.max(top, axis=1, keepdims=True), (TOK, HD))
            if not first:
                before = row_top[h]
                top = jnp.maximum(top, before)
                decay = jnp.exp2((before - top) * EXP2_SCALE)
            row_top[h] = top
            total = None
            for half_pair in range(2):
                weights = [
                    jnp.exp2((tiles[half_pair * 2 + lt] - top) * EXP2_SCALE) for lt in range(2)
                ]
                weights = jnp.concatenate(weights, axis=1)
                gw = nt_dot(g_h, kv[low_slot + half_pair, 1, pl.ds(0, TOK), :])
                both = jnp.concatenate([weights.astype(BF16), (weights * gw).astype(BF16)], axis=0)
                right = jnp.concatenate([kv[low_slot + half_pair, 0, pl.ds(0, TOK), :], ones], axis=1)
                term = jnp.dot(both, right, preferred_element_type=F32)
                total = term if total is None else total + term
            if first:
                acc[h] = total
            else:
                wide = jnp.concatenate([decay, decay], axis=1)
                wide = jnp.concatenate([wide, wide], axis=0)
                acc[h] = acc[h] * wide + total

    get_q.wait()
    get_go.wait()
    await_mine(sib)
    await_other(sib)
    attend(pair, True)

    def event(e):
        e_low = jnp.clip(e, 0, 6)
        e_high = jnp.clip(e - 7, 0, 6)
        code = jnp.where(
            e < 7, lax.shift_right_logical(jnp.int32(EARLY), 4 * e_low),
            jnp.where(e < 14, lax.shift_right_logical(jnp.int32(LATE), 4 * e_high), LAST),
        )
        code = code & 15
        lower, off = div(code, 8), rem(code, 8)
        valid = (e >= 0) & (e < len(ARRIVALS)) & (lower <= y_hi)
        src_pair = (y_hi - lower) * NZ + rem(z + NZ - off, NZ)
        on_plus = valid & ((lax.shift_right_logical(jnp.int32(ON_PLUS), code) & 1) == 1)
        on_minus = valid & ((lax.shift_right_logical(jnp.int32(ON_MINUS), code) & 1) == 1)
        return valid, src_pair, on_plus, on_minus

    @pl.loop(0, len(ARRIVALS) + LAG_USE)
    def _(e):
        valid, src_pair, on_plus, on_minus = event(e)
        chunk = src_pair * 2 + core

        @pl.when(valid)
        def _():
            await_mine(chunk)

            @pl.when(on_plus)
            def _():
                along(chunk, plus_send, z_plus).start()

            @pl.when(on_minus)
            def _():
                along(chunk, minus_send, z_minus).start()

            swap(chunk, 0, x_plus).start()
            swap(chunk, HALF, x_minus).start()
            along(chunk, sib_send, sib).start()

        whole, last_pair, _, _ = event(e - LAG_USE)

        @pl.when(whole)
        def _():
            await_mine(last_pair * 2 + 1 - core)
            await_other(last_pair * 2 + 1 - core)

        @pl.when(whole & (last_pair < pair))
        def _():
            attend(last_pair, False)

        ready, src_pair, _, _ = event(e - LAG_SWAP)
        chunk2 = src_pair * 2 + core

        @pl.when(ready)
        def _():
            await_other(chunk2)
            rest_to_sib(chunk2).start()

    b_all(b_recv).wait()
    own_b.wait()
    b_share().start()

    for h in range(2):
        total = acc[h, pl.ds(0, TOK), pl.ds(HD, HD)]
        inv = 1.0 / total
        delta = acc[h, pl.ds(TOK, TOK), pl.ds(HD, HD)] * inv
        grad = (acc[h, pl.ds(TOK, TOK), pl.ds(0, HD)] - delta * acc[h, pl.ds(0, TOK), pl.ds(0, HD)]) * inv
        gq_ref[:, h * HD : (h + 1) * HD] = (grad * HD ** (-0.5)).astype(BF16)

    gq = gq_ref[...]
    partial = jnp.dot(lowt[...], gq, preferred_element_type=F32) * 2.0
    for h in range(2):
        pbuf[h] = partial[:, h * HD : (h + 1) * HD].reshape(N_ADP, 8, HD)

    def p_copy(i):
        ctx, adp = to_sum(i)
        return pltpu.make_async_remote_copy(
            src_ref=pbuf.at[rem(i, 2), adp], dst_ref=qbuf.at[c],
            send_sem=p_send, recv_sem=p_recv,
            device_id={"ctx": ctx, "adp": adp}, device_id_type=MESH,
        )

    @pl.loop(0, N_CTX)
    def _(i):
        @pl.when(jnp.logical_not(is_self(i)))
        def _():
            p_copy(i).start()

    @pl.when(selfdest == 1)
    def _():
        qbuf[c] = pbuf[core, a]

    out_gq = pltpu.make_async_copy(gq_ref, gq_hbm, out_sem.at[0])
    out_gq.start()

    b_shared().wait()
    for blk in range(2):
        chosen = bcols[bt_ref[blk]]
        padded = jnp.concatenate([chosen, jnp.zeros_like(chosen)], axis=0)
        part = nt_dot(gq[blk * HD : (blk + 1) * HD, :], padded) * 2.0
        rsend[pl.ds(blk * 8, 8)] = part.reshape(8, 16, HD)

    def r_copy(i):
        to = rem(a + i, N_ADP)
        return pltpu.make_async_remote_copy(
            src_ref=rsend.at[to], dst_ref=rbuf.at[a], send_sem=r_send, recv_sem=r_recv,
            device_id={"ctx": c, "adp": to}, device_id_type=MESH,
        )

    def r_all(sem):
        ref = rbuf.at[pl.ds(0, N_ADP - 1)]
        return pltpu.make_async_copy(ref, ref, sem)

    @pl.loop(1, N_ADP)
    def _(i):
        r_copy(i).start()

    rbuf[a] = rsend[a]

    wait_all(btile, bt_recv)
    wait_all(btile, bt_send)
    b_all(b_send).wait()
    b_share().wait_send()
    along(c, plus_send, z_plus).wait_send()
    along(c, minus_send, z_minus).wait_send()
    along(c, sib_send, sib).wait_send()
    rest_to_sib(c).wait_send()

    far(0).wait_send()
    far(1).wait_send()

    @pl.when(y_hi == 0)
    def _():
        for which in range(len(Y_STEPS)):
            to_y(which).wait_send()

    @pl.loop(0, len(ARRIVALS))
    def _(e):
        valid, src_pair, on_plus, on_minus = event(e)
        chunk = src_pair * 2 + core

        @pl.when(on_plus)
        def _():
            along(chunk, plus_send, z_plus).wait_send()

        @pl.when(on_minus)
        def _():
            along(chunk, minus_send, z_minus).wait_send()

        @pl.when(valid)
        def _():
            await_swap_sent(chunk)
            along(chunk, sib_send, sib).wait_send()
            rest_to_sib(chunk).wait_send()

    wait_all(qbuf, p_recv)
    upper = lax.broadcasted_iota(jnp.int32, (8, HD), 0) < 4

    def add_source(i, sums):
        tile = qbuf[i]
        owner = jnp.where(
            upper, jnp.broadcast_to(btile[i, 0:1, :], (8, HD)), jnp.broadcast_to(btile[i, 1:2, :], (8, HD))
        )
        return tuple(s + jnp.where(owner == t, tile, 0.0) for t, s in enumerate(sums))

    sums = lax.fori_loop(0, N_CTX, add_source, tuple(jnp.zeros((8, HD), F32) for _ in range(N_ADP)))
    for t in range(N_ADP):
        tbuf[t] = sums[t]

    def g_copy(i):
        to = rem(a + i, N_ADP)
        return pltpu.make_async_remote_copy(
            src_ref=tbuf.at[to], dst_ref=gbuf.at[a], send_sem=g_send, recv_sem=g_recv,
            device_id={"ctx": c, "adp": to}, device_id_type=MESH,
        )

    def g_all(sem):
        ref = gbuf.at[pl.ds(0, N_ADP - 1)]
        return pltpu.make_async_copy(ref, ref, sem)

    @pl.loop(1, N_ADP)
    def _(i):
        g_copy(i).start()

    gbuf[a] = tbuf[a]

    r_all(r_recv).wait()
    share = rbuf[0]
    for i in range(1, N_ADP):
        share = share + rbuf[i]
    glr_ref[...] = share[:, :RANK]
    out_glr = pltpu.make_async_copy(glr_ref, glr_hbm, out_sem.at[1])
    out_glr.start()
    wait_all(qbuf, p_send)
    r_all(r_send).wait()
    out_gq.wait()

    g_all(g_recv).wait()
    for i in range(N_ADP):
        tile = gbuf[i]
        ga_ref[0, pl.ds(i * 4, 4), :] = tile[0:4] + tile[4:8]
    out_ga = pltpu.make_async_copy(ga_ref, ga_hbm, out_sem.at[2])
    out_ga.start()
    g_all(g_send).wait()
    out_glr.wait()
    out_ga.wait()


def finish(gq_in, glr_in, ga_in, gq_out, glr_out, ga_out):
    gq_out[...] = gq_in[...]
    glr_out[...] = glr_in[...]
    ga_out[...] = ga_in[...]


def on_device(queries, keys, values, grad_out, docs, block_tenant, low_rank, adapter_b):
    anywhere = pl.BlockSpec(memory_space=pl.ANY)
    vmem = pl.BlockSpec(memory_space=pltpu.VMEM)
    dma = pltpu.SemaphoreType.DMA
    shapes = (
        jax.ShapeDtypeStruct((TOK, 2 * HD), BF16),
        jax.ShapeDtypeStruct((16, RANK), F32),
        jax.ShapeDtypeStruct((1, RANK, HD), F32),
    )
    grads = pl.pallas_call(
        body,
        out_shape=shapes,
        in_specs=[anywhere] * 8,
        out_specs=(anywhere,) * 3,
        scratch_shapes=[
            pltpu.VMEM((N_CTX, 2, SLOT, HD), BF16),
            pltpu.VMEM((SLOT, HD), BF16),
            pltpu.VMEM((TOK, 2 * HD), BF16),
            pltpu.VMEM((TOK, 2 * HD), BF16),
            pltpu.VMEM((2, HD), jnp.int32),
            pltpu.SMEM((2,), jnp.int32),
            pltpu.VMEM((RANK, TOK), BF16),
            pltpu.VMEM((TOK, 2 * HD), BF16),
            pltpu.VMEM((16, RANK), F32),
            pltpu.VMEM((1, RANK, HD), F32),
            pltpu.VMEM((2, 2 * TOK, 2 * HD), F32),
            pltpu.VMEM((2, TOK, HD), F32),
            pltpu.VMEM((TOK, HD), F32),
            pltpu.VMEM((N_ADP, RANK, 2 * HD), BF16),
            pltpu.VMEM((2, HD), jnp.int32),
            pltpu.VMEM((N_CTX, 2, HD), jnp.int32),
            pltpu.VMEM((2 * RANK, TOK), BF16),
            pltpu.VMEM((2, N_ADP, 8, HD), F32),
            pltpu.VMEM((N_CTX, 8, HD), F32),
            pltpu.VMEM((N_ADP, 8, HD), F32),
            pltpu.VMEM((N_ADP, 8, HD), F32),
            pltpu.VMEM((N_ADP, 16, HD), F32),
            pltpu.VMEM((N_ADP, 16, HD), F32),
            dma((9,)), dma((N_CTX,)), dma((N_CTX,)), dma((N_CTX,)), dma((N_CTX,)),
            dma((N_CTX,)), dma((N_CTX,)), dma((N_CTX,)), dma((len(Y_STEPS),)), dma((2,)),
            dma, dma, dma, dma, dma, dma, dma, dma, dma, dma, dma, dma, dma((3,)),
        ],
        compiler_params=pltpu.CompilerParams(
            collective_id=0, has_side_effects=True, vmem_limit_bytes=60 * 1024 * 1024
        ),
        cost_estimate=pl.CostEstimate(flops=4_000_000_000, bytes_accessed=4_000_000, transcendentals=4_000_000),
    )(
        queries, keys, values, grad_out, docs.reshape(2, HD), block_tenant, low_rank.T, adapter_b
    )
    return pl.pallas_call(
        finish,
        out_shape=shapes,
        in_specs=[vmem] * 3,
        out_specs=(vmem,) * 3,
        compiler_params=pltpu.CompilerParams(vmem_limit_bytes=60 * 1024 * 1024),
    )(*grads)


def solution(mesh):
    placed = (
        P("ctx", "adp"),
        P("ctx", None),
        P("ctx", None),
        P("ctx", "adp"),
        P("ctx"),
        P("ctx"),
        P("ctx", None),
        P("adp", None, None),
    )
    return jax.shard_map(
        on_device,
        mesh=mesh,
        in_specs=placed,
        out_specs=(P("ctx", "adp"), P(("ctx", "adp"), None), P("adp", None, "ctx")),
        check_vma=False,
    )
```

```python
import math

import jax
import jax.numpy as jnp
from jax import lax
from jax.experimental import pallas as pl
from jax.experimental.pallas import tpu as pltpu
from jax.sharding import PartitionSpec as P

HD = 128
RANK = 64
TOK = 256
NZ = 8
NX = 4
NYL = 4
N_CTX = 32
N_ADP = 16
SLOT = TOK + 16
HALF = TOK // 2
EXP2_SCALE = HD ** (-0.5) * math.log2(math.e)
FAR = -1e30
MESH = pl.DeviceIdType.MESH
ARRIVALS = (1, 7, 8 + 0, 2, 6, 8 + 1, 8 + 7, 3, 5, 8 + 2, 8 + 6, 4, 8 + 3, 8 + 5, 8 + 4)
ON_PLUS = sum(1 << code for code in (1, 2, 8, 9, 10, 11))
ON_MINUS = sum(1 << code for code in (7, 6, 5, 8, 15, 14))
Y_STEPS = (0,)
EARLY = sum(code << (4 * i) for i, code in enumerate(ARRIVALS[:7]))
LATE = sum(code << (4 * i) for i, code in enumerate(ARRIVALS[7:14]))
LAST = ARRIVALS[14]
LAG_SWAP, LAG_USE = 2, 4
F32 = jnp.float32
BF16 = jnp.bfloat16


def rem(value, by):
    return lax.rem(value, jnp.int32(by))


def div(value, by):
    return lax.div(value, jnp.int32(by))


def nt_dot(a, b):
    return lax.dot_general(a, b, (((1,), (1,)), ((), ())), preferred_element_type=F32)


def body(
    q_hbm, k_hbm, v_hbm, go_hbm, docs_hbm, bt_hbm, low_hbm, b_hbm,
    gq_hbm, glr_hbm, ga_hbm,
    kv, xkv, q_ref, go_ref, docs_ref, bt_ref, low_ref, gq_ref, glr_ref, ga_ref,
    acc, row_top, qdoc, bcols, bt_mine, btile, lowt, pbuf, qbuf, tbuf, gbuf, rsend, rbuf,
    loc_sem, mine_recv, other_recv, plus_send, minus_send, sib_send, sib2_send, x_send, y_send,
    bt_recv, bt_send, b_recv, b_send, bs_recv, bs_send,
    r_recv, r_send, p_recv, p_send, g_recv, g_send, out_sem,
):
    c = lax.axis_index("ctx")
    a = lax.axis_index("adp")
    core = rem(c, 2)
    pair = div(c, 2)
    z = rem(pair, NZ)
    y_hi = div(pair, NZ)
    head = div(a, NX)
    x = rem(a, NX)
    mine = rem(x, 2)
    other = 1 - mine
    sib = pair * 2 + (1 - core)
    z_plus = (y_hi * NZ + rem(z + 1, NZ)) * 2 + core
    z_minus = (y_hi * NZ + rem(z + NZ - 1, NZ)) * 2 + core
    x_plus = head * NX + rem(x + 1, NX)
    x_minus = head * NX + rem(x + NX - 1, NX)

    def y_ctx(step):
        return ((1 - y_hi) * NZ + rem(z + NZ + step, NZ)) * 2 + core

    y_adp = (NYL - 1 - head) * NX + x
    selfdest = (pair == a).astype(jnp.int32)

    barrier = pltpu.get_barrier_semaphore()

    def greet(ctx, adp):
        pl.semaphore_signal(barrier, inc=1, device_id={"ctx": ctx, "adp": adp}, device_id_type=MESH)

    greet(z_plus, a)
    greet(z_minus, a)
    greet(sib, a)

    @pl.when(y_hi == 1)
    def _():
        for step in Y_STEPS:
            greet(y_ctx(step), y_adp)

    @pl.loop(1, N_ADP)
    def _(i):
        greet(c, rem(a + i, N_ADP))

    @pl.loop(0, N_CTX)
    def _(i):
        @pl.when(jnp.logical_not((pair == a) & (i == c)))
        def _():
            greet(i, pair)

    def col(which):
        return pl.ds(pl.multiple_of(which * HD, HD), HD)

    far_head = NYL - 1 - head
    get_docs = pltpu.make_async_copy(docs_hbm, docs_ref, loc_sem.at[0])
    own_k = pltpu.make_async_copy(k_hbm.at[:, col(head)], kv.at[c, 0, pl.ds(0, TOK)], loc_sem.at[1])
    own_v = pltpu.make_async_copy(v_hbm.at[:, col(head)], kv.at[c, 1, pl.ds(0, TOK)], loc_sem.at[2])
    x_k = pltpu.make_async_copy(k_hbm.at[:, col(far_head)], xkv.at[pl.ds(0, TOK)], loc_sem.at[3])
    x_v = pltpu.make_async_copy(v_hbm.at[:, col(far_head)], xkv.at[pl.ds(0, TOK)], loc_sem.at[3])
    get_q = pltpu.make_async_copy(q_hbm, q_ref, loc_sem.at[4])
    get_go = pltpu.make_async_copy(go_hbm, go_ref, loc_sem.at[5])
    get_bt = pltpu.make_async_copy(bt_hbm, bt_ref, loc_sem.at[6])
    get_low = pltpu.make_async_copy(low_hbm, low_ref, loc_sem.at[7])
    half = pl.multiple_of(core * (RANK // 2), RANK // 2)
    own_b = pltpu.make_async_copy(
        b_hbm.at[0, pl.ds(half, RANK // 2), pl.ds(pl.multiple_of(a * 2 * HD, 2 * HD), 2 * HD)],
        bcols.at[a, pl.ds(half, RANK // 2)],
        loc_sem.at[8],
    )
    get_docs.start()
    own_k.start()
    own_v.start()

    @pl.when(mine == 0)
    def _():
        x_k.start()

    @pl.when(mine == 1)
    def _():
        x_v.start()

    get_bt.start()
    get_q.start()
    get_go.start()
    get_low.start()
    own_b.start()

    get_docs.wait()
    doc_rows = docs_ref[...].astype(F32)
    tag = jnp.concatenate([doc_rows, jnp.zeros((14, HD), F32)], axis=0).astype(BF16)
    kv[c, mine, pl.ds(TOK, 16), :] = tag
    xkv[pl.ds(TOK, 16), :] = tag
    own_k.wait()
    own_v.wait()
    x_k.wait()
    pl.semaphore_wait(barrier, 3 + len(Y_STEPS) * (1 - y_hi) + (N_ADP - 1) + N_CTX - selfdest)

    def along(chunk, send_sem, to):
        ref = kv.at[chunk, mine]
        return pltpu.make_async_remote_copy(
            src_ref=ref, dst_ref=ref, send_sem=send_sem.at[chunk], recv_sem=mine_recv.at[chunk],
            device_id={"ctx": to, "adp": a}, device_id_type=MESH,
        )

    def rest_to_sib(chunk):
        ref = kv.at[chunk, other, pl.ds(0, TOK)]
        return pltpu.make_async_remote_copy(
            src_ref=ref, dst_ref=ref, send_sem=sib2_send.at[chunk], recv_sem=other_recv.at[chunk],
            device_id={"ctx": sib, "adp": a}, device_id_type=MESH,
        )

    def swap(chunk, first, to):
        ref = kv.at[chunk, mine, pl.ds(first, HALF)]
        return pltpu.make_async_remote_copy(
            src_ref=ref, dst_ref=ref, send_sem=x_send.at[chunk], recv_sem=other_recv.at[chunk],
            device_id={"ctx": c, "adp": to}, device_id_type=MESH,
        )

    def to_y(which):
        return pltpu.make_async_remote_copy(
            src_ref=xkv, dst_ref=kv.at[c, mine], send_sem=y_send.at[which], recv_sem=mine_recv.at[c],
            device_id={"ctx": y_ctx(Y_STEPS[which]), "adp": y_adp}, device_id_type=MESH,
        )

    def await_mine(chunk):
        ref = kv.at[chunk, mine]
        pltpu.make_async_copy(ref, ref, mine_recv.at[chunk]).wait()

    def await_other(chunk):
        ref = kv.at[chunk, other, pl.ds(0, TOK)]
        pltpu.make_async_copy(ref, ref, other_recv.at[chunk]).wait()

    def await_swap_sent(chunk):
        ref = kv.at[chunk, mine, pl.ds(0, TOK)]
        pltpu.make_async_copy(ref, ref, x_send.at[chunk]).wait()

    along(c, plus_send, z_plus).start()
    along(c, minus_send, z_minus).start()


    @pl.when(y_hi == 0)
    def _():
        for which in range(len(Y_STEPS)):
            to_y(which).start()

    along(c, sib_send, sib).start()
    rest_to_sib(c).start()

    def b_copy(i):
        to = rem(a + i, N_ADP)
        return pltpu.make_async_remote_copy(
            src_ref=b_hbm.at[0, pl.ds(half, RANK // 2), pl.ds(pl.multiple_of(to * 2 * HD, 2 * HD), 2 * HD)],
            dst_ref=bcols.at[a, pl.ds(half, RANK // 2)],
            send_sem=b_send, recv_sem=b_recv,
            device_id={"ctx": c, "adp": to}, device_id_type=MESH,
        )

    def b_all(sem):
        ref = bcols.at[pl.ds(0, N_ADP - 1), pl.ds(half, RANK // 2)]
        return pltpu.make_async_copy(ref, ref, sem)

    def b_share():
        ref = bcols.at[:, pl.ds(half, RANK // 2)]
        return pltpu.make_async_remote_copy(
            src_ref=ref, dst_ref=ref, send_sem=bs_send, recv_sem=bs_recv,
            device_id={"ctx": sib, "adp": a}, device_id_type=MESH,
        )

    def b_shared():
        ref = bcols.at[:, pl.ds(pl.multiple_of((1 - core) * (RANK // 2), RANK // 2), RANK // 2)]
        return pltpu.make_async_copy(ref, ref, bs_recv)

    @pl.loop(1, N_ADP)
    def _(i):
        b_copy(i).start()

    get_bt.wait()
    bt_mine[...] = jnp.where(lax.broadcasted_iota(jnp.int32, (2, HD), 0) == 0, bt_ref[0], bt_ref[1])

    def to_sum(i):
        return a * 2 + rem(i, 2), rem(a + div(i, 2), N_ADP)

    def bt_copy(i):
        ctx, adp = to_sum(i)
        return pltpu.make_async_remote_copy(
            src_ref=bt_mine, dst_ref=btile.at[c], send_sem=bt_send, recv_sem=bt_recv,
            device_id={"ctx": ctx, "adp": adp}, device_id_type=MESH,
        )

    def wait_all(buffer, sem):
        @pl.when(selfdest == 0)
        def _():
            pltpu.make_async_copy(buffer, buffer, sem).wait()

        @pl.when(selfdest == 1)
        def _():
            ref = buffer.at[pl.ds(0, N_CTX - 1)]
            pltpu.make_async_copy(ref, ref, sem).wait()

    def is_self(i):
        return (selfdest == 1) & (i == core)

    @pl.loop(0, N_CTX)
    def _(i):
        @pl.when(jnp.logical_not(is_self(i)))
        def _():
            bt_copy(i).start()

    @pl.when(selfdest == 1)
    def _():
        btile[c] = bt_mine[...]

    get_low.wait()
    rr = lax.broadcasted_iota(jnp.int32, (2 * RANK, RANK), 0)
    kk = lax.broadcasted_iota(jnp.int32, (2 * RANK, RANK), 1)
    pick = jnp.where(kk == ((rr >> 3) * 4 + (rr & 3)), 1.0, 0.0).astype(BF16)
    spread = jnp.dot(pick, low_ref[...], preferred_element_type=F32)
    rr = lax.broadcasted_iota(jnp.int32, (2 * RANK, TOK), 0)
    tt = lax.broadcasted_iota(jnp.int32, (2 * RANK, TOK), 1)
    lowt[...] = jnp.where((tt >> 7) == ((rr >> 2) & 1), spread, 0.0).astype(BF16)

    ri = lax.broadcasted_iota(jnp.int32, (HD, HD), 0)
    ci = lax.broadcasted_iota(jnp.int32, (HD, HD), 1)
    for part in range(2):
        spot = jnp.where(ri == ci, jnp.broadcast_to(doc_rows[part : part + 1, :], (HD, HD)), 0.0)
        column = jnp.sum(spot, axis=1, keepdims=True)
        qdoc[pl.ds(part * HD, HD), :] = jnp.broadcast_to(column, (HD, HD))

    ones = jnp.ones((TOK, HD), BF16)

    def attend(which, first):
        low_slot = which * 2
        row_doc = qdoc[...]
        for h in range(2):
            q_h = q_ref[:, h * HD : (h + 1) * HD]
            g_h = go_ref[:, h * HD : (h + 1) * HD]
            tiles = []
            for half_pair in range(2):
                scores = nt_dot(q_h, kv[low_slot + half_pair, 0, pl.ds(0, TOK), :])
                key_doc = kv[low_slot + half_pair, mine, pl.ds(TOK, 16), :].astype(F32)
                for lt in range(2):
                    seen = row_doc == key_doc[lt : lt + 1, :]
                    if first:
                        rpos = lax.broadcasted_iota(jnp.int32, (TOK, HD), 0) + core * TOK
                        kpos = lax.broadcasted_iota(jnp.int32, (TOK, HD), 1) + (half_pair * TOK + lt * HD)
                        seen = seen & (kpos <= rpos)
                    tiles.append(jnp.where(seen, scores[:, lt * HD : (lt + 1) * HD], FAR))
            top = jnp.maximum(jnp.maximum(tiles[0], tiles[1]), jnp.maximum(tiles[2], tiles[3]))
            top = jnp.broadcast_to(jnp.max(top, axis=1, keepdims=True), (TOK, HD))
            if not first:
                before = row_top[h]
                top = jnp.maximum(top, before)
                decay = jnp.exp2((before - top) * EXP2_SCALE)
            row_top[h] = top
            total = None
            for half_pair in range(2):
                weights = [
                    jnp.exp2((tiles[half_pair * 2 + lt] - top) * EXP2_SCALE) for lt in range(2)
                ]
                weights = jnp.concatenate(weights, axis=1)
                gw = nt_dot(g_h, kv[low_slot + half_pair, 1, pl.ds(0, TOK), :])
                both = jnp.concatenate([weights.astype(BF16), (weights * gw).astype(BF16)], axis=0)
                right = jnp.concatenate([kv[low_slot + half_pair, 0, pl.ds(0, TOK), :], ones], axis=1)
                term = jnp.dot(both, right, preferred_element_type=F32)
                total = term if total is None else total + term
            if first:
                acc[h] = total
            else:
                wide = jnp.concatenate([decay, decay], axis=1)
                wide = jnp.concatenate([wide, wide], axis=0)
                acc[h] = acc[h] * wide + total

    get_q.wait()
    get_go.wait()
    await_mine(sib)
    await_other(sib)
    attend(pair, True)

    def event(e):
        e_low = jnp.clip(e, 0, 6)
        e_high = jnp.clip(e - 7, 0, 6)
        code = jnp.where(
            e < 7, lax.shift_right_logical(jnp.int32(EARLY), 4 * e_low),
            jnp.where(e < 14, lax.shift_right_logical(jnp.int32(LATE), 4 * e_high), LAST),
        )
        code = code & 15
        lower, off = div(code, 8), rem(code, 8)
        valid = (e >= 0) & (e < len(ARRIVALS)) & (lower <= y_hi)
        src_pair = (y_hi - lower) * NZ + rem(z + NZ - off, NZ)
        on_plus = valid & ((lax.shift_right_logical(jnp.int32(ON_PLUS), code) & 1) == 1)
        on_minus = valid & ((lax.shift_right_logical(jnp.int32(ON_MINUS), code) & 1) == 1)
        return valid, src_pair, on_plus, on_minus

    @pl.loop(0, len(ARRIVALS) + LAG_USE)
    def _(e):
        valid, src_pair, on_plus, on_minus = event(e)
        chunk = src_pair * 2 + core

        @pl.when(valid)
        def _():
            await_mine(chunk)

            @pl.when(on_plus)
            def _():
                along(chunk, plus_send, z_plus).start()

            @pl.when(on_minus)
            def _():
                along(chunk, minus_send, z_minus).start()

            swap(chunk, 0, x_plus).start()
            swap(chunk, HALF, x_minus).start()
            along(chunk, sib_send, sib).start()

        whole, last_pair, _, _ = event(e - LAG_USE)

        @pl.when(whole)
        def _():
            await_mine(last_pair * 2 + 1 - core)
            await_other(last_pair * 2 + 1 - core)

        @pl.when(whole & (last_pair < pair))
        def _():
            attend(last_pair, False)

        ready, src_pair, _, _ = event(e - LAG_SWAP)
        chunk2 = src_pair * 2 + core

        @pl.when(ready)
        def _():
            await_other(chunk2)
            rest_to_sib(chunk2).start()

    b_all(b_recv).wait()
    own_b.wait()
    b_share().start()

    for h in range(2):
        total = acc[h, pl.ds(0, TOK), pl.ds(HD, HD)]
        inv = 1.0 / total
        delta = acc[h, pl.ds(TOK, TOK), pl.ds(HD, HD)] * inv
        grad = (acc[h, pl.ds(TOK, TOK), pl.ds(0, HD)] - delta * acc[h, pl.ds(0, TOK), pl.ds(0, HD)]) * inv
        gq_ref[:, h * HD : (h + 1) * HD] = (grad * HD ** (-0.5)).astype(BF16)

    gq = gq_ref[...]
    partial = jnp.dot(lowt[...], gq, preferred_element_type=F32) * 2.0
    for h in range(2):
        pbuf[h] = partial[:, h * HD : (h + 1) * HD].reshape(N_ADP, 8, HD)

    def p_copy(i):
        ctx, adp = to_sum(i)
        return pltpu.make_async_remote_copy(
            src_ref=pbuf.at[rem(i, 2), adp], dst_ref=qbuf.at[c],
            send_sem=p_send, recv_sem=p_recv,
            device_id={"ctx": ctx, "adp": adp}, device_id_type=MESH,
        )

    @pl.loop(0, N_CTX)
    def _(i):
        @pl.when(jnp.logical_not(is_self(i)))
        def _():
            p_copy(i).start()

    @pl.when(selfdest == 1)
    def _():
        qbuf[c] = pbuf[core, a]

    out_gq = pltpu.make_async_copy(gq_ref, gq_hbm, out_sem.at[0])
    out_gq.start()

    b_shared().wait()
    for blk in range(2):
        chosen = bcols[bt_ref[blk]]
        padded = jnp.concatenate([chosen, jnp.zeros_like(chosen)], axis=0)
        part = nt_dot(gq[blk * HD : (blk + 1) * HD, :], padded) * 2.0
        rsend[pl.ds(blk * 8, 8)] = part.reshape(8, 16, HD)

    def r_copy(i):
        to = rem(a + i, N_ADP)
        return pltpu.make_async_remote_copy(
            src_ref=rsend.at[to], dst_ref=rbuf.at[a], send_sem=r_send, recv_sem=r_recv,
            device_id={"ctx": c, "adp": to}, device_id_type=MESH,
        )

    def r_all(sem):
        ref = rbuf.at[pl.ds(0, N_ADP - 1)]
        return pltpu.make_async_copy(ref, ref, sem)

    @pl.loop(1, N_ADP)
    def _(i):
        r_copy(i).start()

    rbuf[a] = rsend[a]

    wait_all(btile, bt_recv)
    wait_all(btile, bt_send)
    b_all(b_send).wait()
    b_share().wait_send()
    along(c, plus_send, z_plus).wait_send()
    along(c, minus_send, z_minus).wait_send()
    along(c, sib_send, sib).wait_send()
    rest_to_sib(c).wait_send()


    @pl.when(y_hi == 0)
    def _():
        for which in range(len(Y_STEPS)):
            to_y(which).wait_send()

    @pl.loop(0, len(ARRIVALS))
    def _(e):
        valid, src_pair, on_plus, on_minus = event(e)
        chunk = src_pair * 2 + core

        @pl.when(on_plus)
        def _():
            along(chunk, plus_send, z_plus).wait_send()

        @pl.when(on_minus)
        def _():
            along(chunk, minus_send, z_minus).wait_send()

        @pl.when(valid)
        def _():
            await_swap_sent(chunk)
            along(chunk, sib_send, sib).wait_send()
            rest_to_sib(chunk).wait_send()

    wait_all(qbuf, p_recv)
    upper = lax.broadcasted_iota(jnp.int32, (8, HD), 0) < 4

    def add_source(i, sums):
        tile = qbuf[i]
        owner = jnp.where(
            upper, jnp.broadcast_to(btile[i, 0:1, :], (8, HD)), jnp.broadcast_to(btile[i, 1:2, :], (8, HD))
        )
        return tuple(s + jnp.where(owner == t, tile, 0.0) for t, s in enumerate(sums))

    sums = lax.fori_loop(0, N_CTX, add_source, tuple(jnp.zeros((8, HD), F32) for _ in range(N_ADP)))
    for t in range(N_ADP):
        tbuf[t] = sums[t]

    def g_copy(i):
        to = rem(a + i, N_ADP)
        return pltpu.make_async_remote_copy(
            src_ref=tbuf.at[to], dst_ref=gbuf.at[a], send_sem=g_send, recv_sem=g_recv,
            device_id={"ctx": c, "adp": to}, device_id_type=MESH,
        )

    def g_all(sem):
        ref = gbuf.at[pl.ds(0, N_ADP - 1)]
        return pltpu.make_async_copy(ref, ref, sem)

    @pl.loop(1, N_ADP)
    def _(i):
        g_copy(i).start()

    gbuf[a] = tbuf[a]

    r_all(r_recv).wait()
    share = rbuf[0]
    for i in range(1, N_ADP):
        share = share + rbuf[i]
    glr_ref[...] = share[:, :RANK]
    out_glr = pltpu.make_async_copy(glr_ref, glr_hbm, out_sem.at[1])
    out_glr.start()
    wait_all(qbuf, p_send)
    r_all(r_send).wait()
    out_gq.wait()

    g_all(g_recv).wait()
    for i in range(N_ADP):
        tile = gbuf[i]
        ga_ref[0, pl.ds(i * 4, 4), :] = tile[0:4] + tile[4:8]
    out_ga = pltpu.make_async_copy(ga_ref, ga_hbm, out_sem.at[2])
    out_ga.start()
    g_all(g_send).wait()
    out_glr.wait()
    out_ga.wait()


def finish(gq_in, glr_in, ga_in, gq_out, glr_out, ga_out):
    gq_out[...] = gq_in[...]
    glr_out[...] = glr_in[...]
    ga_out[...] = ga_in[...]


def on_device(queries, keys, values, grad_out, docs, block_tenant, low_rank, adapter_b):
    anywhere = pl.BlockSpec(memory_space=pl.ANY)
    vmem = pl.BlockSpec(memory_space=pltpu.VMEM)
    dma = pltpu.SemaphoreType.DMA
    shapes = (
        jax.ShapeDtypeStruct((TOK, 2 * HD), BF16),
        jax.ShapeDtypeStruct((16, RANK), F32),
        jax.ShapeDtypeStruct((1, RANK, HD), F32),
    )
    grads = pl.pallas_call(
        body,
        out_shape=shapes,
        in_specs=[anywhere] * 8,
        out_specs=(anywhere,) * 3,
        scratch_shapes=[
            pltpu.VMEM((N_CTX, 2, SLOT, HD), BF16),
            pltpu.VMEM((SLOT, HD), BF16),
            pltpu.VMEM((TOK, 2 * HD), BF16),
            pltpu.VMEM((TOK, 2 * HD), BF16),
            pltpu.VMEM((2, HD), jnp.int32),
            pltpu.SMEM((2,), jnp.int32),
            pltpu.VMEM((RANK, TOK), BF16),
            pltpu.VMEM((TOK, 2 * HD), BF16),
            pltpu.VMEM((16, RANK), F32),
            pltpu.VMEM((1, RANK, HD), F32),
            pltpu.VMEM((2, 2 * TOK, 2 * HD), F32),
            pltpu.VMEM((2, TOK, HD), F32),
            pltpu.VMEM((TOK, HD), F32),
            pltpu.VMEM((N_ADP, RANK, 2 * HD), BF16),
            pltpu.VMEM((2, HD), jnp.int32),
            pltpu.VMEM((N_CTX, 2, HD), jnp.int32),
            pltpu.VMEM((2 * RANK, TOK), BF16),
            pltpu.VMEM((2, N_ADP, 8, HD), F32),
            pltpu.VMEM((N_CTX, 8, HD), F32),
            pltpu.VMEM((N_ADP, 8, HD), F32),
            pltpu.VMEM((N_ADP, 8, HD), F32),
            pltpu.VMEM((N_ADP, 16, HD), F32),
            pltpu.VMEM((N_ADP, 16, HD), F32),
            dma((9,)), dma((N_CTX,)), dma((N_CTX,)), dma((N_CTX,)), dma((N_CTX,)),
            dma((N_CTX,)), dma((N_CTX,)), dma((N_CTX,)), dma((len(Y_STEPS),)),
            dma, dma, dma, dma, dma, dma, dma, dma, dma, dma, dma, dma, dma((3,)),
        ],
        compiler_params=pltpu.CompilerParams(
            collective_id=0, has_side_effects=True, vmem_limit_bytes=60 * 1024 * 1024
        ),
        cost_estimate=pl.CostEstimate(flops=4_000_000_000, bytes_accessed=4_000_000, transcendentals=4_000_000),
    )(
        queries, keys, values, grad_out, docs.reshape(2, HD), block_tenant, low_rank.T, adapter_b
    )
    return pl.pallas_call(
        finish,
        out_shape=shapes,
        in_specs=[vmem] * 3,
        out_specs=(vmem,) * 3,
        compiler_params=pltpu.CompilerParams(vmem_limit_bytes=60 * 1024 * 1024),
    )(*grads)


def solution(mesh):
    placed = (
        P("ctx", "adp"),
        P("ctx", None),
        P("ctx", None),
        P("ctx", "adp"),
        P("ctx"),
        P("ctx"),
        P("ctx", None),
        P("adp", None, None),
    )
    return jax.shard_map(
        on_device,
        mesh=mesh,
        in_specs=placed,
        out_specs=(P("ctx", "adp"), P(("ctx", "adp"), None), P("adp", None, "ctx")),
        check_vma=False,
    )
```
